256 devices in a mesh: leaf: 128 (over x, y, z), sep: 2 (over core).
Axes of the slice: x: 4, y: 4, z: 8, core: 2. Of those that a mesh axis runs over, the one named last changes fastest.
Arguments:
- leaf_rhs: float32 [128, 16, 2048], P('leaf', None, 'sep'), may hold values from -6 to 6
- leaf_inverse: float32 [128, 2048, 2048], P('leaf', 'sep'), may hold values from -0.125 to 0.125
- skeleton_index: int32 [128, 3, 128], P('leaf'), may hold values from 0 to 2047, as said below
- leaf_coupling: float32 [128, 3, 128, 128], P('leaf'), may hold values from -0.046875 to 0.046875
- sep_rhs: float32 [7, 16, 128], replicated, may hold values from -6 to 6
- sep_inverse: float32 [7, 128, 128], replicated, may hold values from -0.5 to 0.5
- sep_parent: float32 [6, 128, 128], replicated, may hold values from -0.5 to 0.5
Outputs:
- leaf_solution: float32 [128, 16, 2048], P('leaf', None, 'sep')
- sep_solution: float32 [128, 3, 16, 128], P('leaf')
The draws below stay inside these ranges and needn't reach their ends.
Inputs may be any that keep to these rules, and one draw needn't show every extreme that they name: `skeleton_index`: the 128 rows of one leaf and level are distinct.
All inputs are finite; a program needn't handle non-finite values.
Results may differ from the reference program's by a relative error of at most 0.0001.
Values sent between devices are 32-bit elements; how exact they have to be, the bound alone decides.
No kernel may reach another device: no remote copies, remote signals or barrier semaphores. Data moves between devices by JAX's collectives and lax.ppermute only.
A program may use at most 64 MiB of HBM per device.

```python
import jax
import jax.numpy as jnp
from jax import lax

K = 128
NRHS = 16
LEVELS = 3
LR = 2048
LEAVES = 128
NSEP = 7
N_LEAF = 128


def draw_skeleton_index(key, part):
    key = jax.random.fold_in(key, 11)
    keys = jax.random.split(key, LEAVES * LEVELS)
    chosen = jax.vmap(lambda single: jax.random.permutation(single, LR)[:K])(keys)
    return chosen.reshape(LEAVES, LEVELS, K).astype(jnp.int32)


def steps_of(key, extent, cuts, smallest, largest):
    gain, own = 1.0, jax.random.fold_in(key, 6)
    for position, blocks in cuts:
        steps = jnp.exp(jax.random.uniform(jax.random.fold_in(own, position), (blocks,), jnp.float32, smallest / len(cuts), largest / len(cuts)))
        gain = gain * jnp.repeat(steps, extent[position] // blocks).reshape([-1 if axis == position else 1 for axis in range(len(extent))])
    return gain


def centred(rng, extent, deviation, limit, shards=(), dtype=jnp.bfloat16):
    gain = steps_of(rng, extent, shards, -0.22, 0.18) if shards else 1.0
    result = jax.random.normal(rng, extent, jnp.float32) * deviation * gain
    return jnp.minimum(jnp.maximum(result, -limit), limit).astype(dtype)


def setup_inputs(seed: int = 0) -> dict:
    seeds = jax.random.split(jax.random.key(seed), 8)
    leaf_rhs = centred(seeds[0], (LEAVES, NRHS, LR), 1.0, 6.0, ((0, 128), (2, 2)), jnp.float32)
    leaf_inverse = centred(seeds[1], (LEAVES, LR, LR), LR ** -0.5, 0.125, ((0, 128), (1, 2)), jnp.float32)
    skeleton_index = draw_skeleton_index(jax.random.fold_in(seeds[7], 71), 0)
    leaf_coupling = centred(seeds[3], (LEAVES, LEVELS, K, K), (K * LEAVES) ** -0.5, 0.046875, ((0, 128),), jnp.float32)
    sep_rhs = centred(seeds[4], (NSEP, NRHS, K), 1.0, 6.0, (), jnp.float32)
    sep_inverse = centred(seeds[5], (NSEP, K, K), K ** -0.5, 0.5, (), jnp.float32)
    sep_parent = centred(seeds[6], (NSEP - 1, K, K), K ** -0.5, 0.5, (), jnp.float32)
    return dict(leaf_rhs=leaf_rhs, leaf_inverse=leaf_inverse, skeleton_index=skeleton_index, leaf_coupling=leaf_coupling, sep_rhs=sep_rhs, sep_inverse=sep_inverse, sep_parent=sep_parent)


HIGH = lax.Precision.HIGHEST


def reference(leaf_rhs, leaf_inverse, skeleton_index, leaf_coupling, sep_rhs, sep_inverse, sep_parent):
    u = jnp.einsum('irc,inc->inr', leaf_inverse, leaf_rhs, precision=HIGH)
    flat_index = skeleton_index.reshape(N_LEAF, LEVELS * K)
    picked = jax.vmap(lambda rows, where: rows[:, where])(u, flat_index).reshape(N_LEAF, NRHS, LEVELS, K)
    term = jnp.einsum('iljk,inlk->ilnj', leaf_coupling, picked, precision=HIGH)
    forward = []
    for level in range(LEVELS):
        width = N_LEAF // 2 ** (LEVELS - 1 - level)
        groups = N_LEAF // width
        offset = 2 ** LEVELS - 2 ** (LEVELS - level)
        summed = term[:, level].reshape(groups, width, NRHS, K).sum(1)
        source = sep_rhs[offset:offset + groups] - summed
        if level > 0:
            lower = 2 ** LEVELS - 2 ** (LEVELS - level + 1)
            parted = jnp.einsum('gjk,gnk->gnj', sep_parent[lower:lower + 2 * groups], forward[-1], precision=HIGH)
            source = source - parted.reshape(groups, 2, NRHS, K).sum(1)
        forward.append(jnp.einsum('gjk,gnk->gnj', sep_inverse[offset:offset + groups], source, precision=HIGH))
    backward = [None] * LEVELS
    for level in reversed(range(LEVELS)):
        width = N_LEAF // 2 ** (LEVELS - 1 - level)
        groups = N_LEAF // width
        offset = 2 ** LEVELS - 2 ** (LEVELS - level)
        target = forward[level]
        if level < LEVELS - 1:
            upper = jnp.repeat(backward[level + 1], 2, axis=0)
            target = target - jnp.einsum('gjk,gnj->gnk', sep_parent[offset:offset + groups], upper, precision=HIGH)
        backward[level] = jnp.einsum('gjk,gnj->gnk', sep_inverse[offset:offset + groups], target, precision=HIGH)
    spread = []
    for level in range(LEVELS):
        width = N_LEAF // 2 ** (LEVELS - 1 - level)
        spread.append(jnp.repeat(backward[level], width, axis=0))
    sep_solution = jnp.stack(spread, axis=1)
    correction = jnp.einsum('iljk,ilnj->inlk', leaf_coupling, sep_solution, precision=HIGH).reshape(N_LEAF, NRHS, LEVELS * K)
    adjusted = jax.vmap(lambda rows, where, extra: rows.at[:, where].add(-extra))(u, flat_index, correction)
    leaf_solution = jnp.einsum('irc,inr->inc', leaf_inverse, adjusted, precision=HIGH)
    return leaf_solution, sep_solution
```

```python
import jax
import jax.numpy as jnp
from jax import lax
from jax.sharding import PartitionSpec as P

HIGH = lax.Precision.HIGHEST


def swap_core(x):
    return lax.ppermute(x, "sep", [(0, 1), (1, 0)])


def swap_leaf(x, mask):
    return lax.ppermute(x, "leaf", [(i, i ^ mask) for i in range(lax.axis_size("leaf"))])


def local(leaf_rhs, leaf_inverse, skeleton_index, leaf_coupling, sep_rhs, sep_inverse, sep_parent):
    n_leaf = lax.axis_size("leaf")
    my_leaf = lax.axis_index("leaf")
    my_side = lax.axis_index("sep")
    levels = skeleton_index.shape[1]
    width_k = sep_rhs.shape[2]
    count_rhs = leaf_rhs.shape[1]
    half = leaf_rhs.shape[2]
    inverse = leaf_inverse[0]
    coupling = leaf_coupling[0]
    mine = leaf_rhs[0]
    theirs = swap_core(mine)
    low = jnp.where(my_side == 0, mine, theirs)
    high = jnp.where(my_side == 0, theirs, mine)
    u_half = jnp.einsum(
        "nc,rc->nr", jnp.concatenate([low, high], axis=1), inverse, precision=HIGH
    )
    local_index = skeleton_index[0] - my_side * half
    inside = ((local_index >= 0) & (local_index < half)).astype(jnp.float32)
    safe_index = jnp.clip(local_index, 0, half - 1).reshape(-1)
    picked = u_half[:, safe_index].reshape(count_rhs, levels, width_k) * inside[None]
    term = jnp.einsum("ljk,nlk->lnj", coupling, picked, precision=HIGH)
    term = term + swap_core(term)
    for mask in (1, 2, 6, 8, 24):
        term = term + swap_leaf(term, mask)
    summed = [term[0]]
    upper = term[1:] + swap_leaf(term[1:], 32)
    summed.append(upper[0])
    summed.append(upper[1] + swap_leaf(upper[1], 96))
    nodes = []
    for level in range(levels):
        nodes.append(2**levels - 2 ** (levels - level) + my_leaf // (n_leaf // 2 ** (levels - 1 - level)))
    forward = []
    for level in range(levels):
        node = nodes[level]
        source = sep_rhs[node] - summed[level]
        if level > 0:
            child = nodes[level - 1]
            own = jnp.einsum("jk,nk->nj", sep_parent[child], forward[-1], precision=HIGH)
            source = source - (own + swap_leaf(own, 32 if level == 1 else 96))
        forward.append(jnp.einsum("jk,nk->nj", sep_inverse[node], source, precision=HIGH))
    backward = [None] * levels
    for level in reversed(range(levels)):
        target = forward[level]
        if level < levels - 1:
            target = target - jnp.einsum(
                "jk,nj->nk", sep_parent[nodes[level]], backward[level + 1], precision=HIGH
            )
        backward[level] = jnp.einsum("jk,nj->nk", sep_inverse[nodes[level]], target, precision=HIGH)
    solved = jnp.stack(backward, axis=0)
    correction = jnp.einsum("ljk,lnj->nlk", coupling, solved, precision=HIGH) * inside[None]
    adjusted = u_half.at[:, safe_index].add(-correction.reshape(count_rhs, levels * width_k))
    result = jnp.einsum("nr,rc->nc", adjusted, inverse, precision=HIGH)
    keep = jnp.where(my_side == 0, result[:, :half], result[:, half:])
    send = jnp.where(my_side == 0, result[:, half:], result[:, :half])
    return ((keep + swap_core(send))[None], solved[None])


def solution(mesh):
    placed = (
        P("leaf", None, "sep"),
        P("leaf", "sep", None),
        P("leaf", None, None),
        P("leaf", None, None, None),
        P(),
        P(),
        P(),
    )
    return jax.shard_map(
        local,
        mesh=mesh,
        in_specs=placed,
        out_specs=(P("leaf", None, "sep"), P("leaf", None, None, None)),
        check_vma=False,
    )
```

```python
import functools

import jax
import jax.numpy as jnp
from jax import lax
from jax.experimental import pallas as pl
from jax.experimental.pallas import tpu as pltpu
from jax.sharding import PartitionSpec as P

F32, BF16 = jnp.float32, jnp.bfloat16
HIGH = lax.Precision.HIGHEST
MIB = 1 << 20
VMEM = pl.BlockSpec(memory_space=pltpu.VMEM)
SMEM = pl.BlockSpec(memory_space=pltpu.SMEM)
HBM = pl.BlockSpec(memory_space=pltpu.HBM)
NN = (((1,), (0,)), ((), ()))
NT = (((1,), (1,)), ((), ()))
TN = (((0,), (0,)), ((), ()))


def shape(*dims, dtype=F32):
    return jax.ShapeDtypeStruct(dims, dtype)


def dot(a, b, dims=NN):
    return lax.dot_general(a, b, dims, preferred_element_type=F32)


def full(a, b, dims=NN):
    return lax.dot_general(a, b, dims, precision=HIGH, preferred_element_type=F32)


def split(x):
    high = x.astype(BF16)
    return high, (x - high.astype(F32)).astype(BF16)


def product(a, split_b, dims=NN):
    ah, al = split(a)
    bh, bl = split_b
    rows = a.shape[0]
    both = dot(jnp.concatenate([ah, al], axis=0), bh, dims)
    return both[:rows] + both[rows:] + dot(ah, bl, dims)


def call(name, body, outs, ins, scratch=(), limit=24):
    return pl.pallas_call(
        body,
        out_shape=outs,
        in_specs=ins,
        out_specs=[VMEM] * len(outs),
        scratch_shapes=list(scratch),
        compiler_params=pltpu.CompilerParams(vmem_limit_bytes=limit * MIB),
        name=name,
    )


def load_columns(inverse_ref, first, steps, chunk, a_ref, sems):
    copies = []
    for s in range(steps):
        start = pl.multiple_of(first + s * chunk, chunk)
        copy = pltpu.make_async_copy(inverse_ref.at[:, pl.ds(start, chunk)], a_ref.at[s], sems.at[s])
        copy.start()
        copies.append(copy)
    return copies


def column_product(copies, chunk, x_ref, a_ref, ah_ref, al_ref):
    n = x_ref.shape[0]
    total = None
    for s, copy in enumerate(copies):
        xh, xl = split(x_ref[:, s * chunk:(s + 1) * chunk])
        x = jnp.concatenate([xh, xl], axis=0)
        copy.wait()
        ah, al = split(a_ref[s])
        ah_ref[s] = ah
        al_ref[s] = al
        part = dot(x, ah, NT) + dot(x, al, NT)
        total = part if total is None else total + part
    return total[:n] + total[n:]


def one_hot(index_ref, level, rows, first):
    row = lax.broadcasted_iota(jnp.int32, (rows, index_ref.shape[1]), 0) + first
    return jnp.where(row == index_ref[level:level + 1, :], 1.0, 0.0).astype(BF16)


def first_kernel(chunk, where_ref, x_ref, inverse_ref, out_ref, ah_ref, al_ref, a_ref, sems):
    half = x_ref.shape[1]
    copies = load_columns(inverse_ref, where_ref[0] * half, half // chunk, chunk, a_ref, sems)
    out_ref[...] = column_product(copies, chunk, x_ref, a_ref, ah_ref, al_ref)


def second_kernel(chunk, where_ref, x_ref, part_ref, index_ref, coupling_ref, inverse_ref, term_ref, u_ref, ah_ref, al_ref, a_ref, sems):
    n, half = x_ref.shape
    levels, k = index_ref.shape
    side = where_ref[0]
    copies = load_columns(inverse_ref, (1 - side) * half, half // chunk, chunk, a_ref, sems)
    hot = [one_hot(index_ref, level, half, side * half) for level in range(levels)]
    u = part_ref[...] + column_product(copies, chunk, x_ref, a_ref, ah_ref, al_ref)
    u_ref[...] = u
    uh, um = split(u)
    ul = (u - uh.astype(F32) - um.astype(F32)).astype(BF16)
    parts = jnp.concatenate([uh, um, ul], axis=0)
    for level in range(levels):
        picked = dot(parts, hot[level])
        picked = picked[:n] + picked[n:2 * n] + picked[2 * n:]
        term_ref[:, level * k:(level + 1) * k] = product(picked, split(coupling_ref[level]), NT)


def spread_kernel(where_ref, index_ref, coupling_ref, high_ref, low_ref):
    levels, k = index_ref.shape
    half = high_ref.shape[1]
    for level in range(levels):
        hot = one_hot(index_ref, level, half, where_ref[0] * half)
        ch, cl = split(coupling_ref[level])
        moved = dot(jnp.concatenate([ch, cl], axis=0), hot, NT).astype(BF16)
        high_ref[level * k:(level + 1) * k, :] = moved[:k]
        low_ref[level * k:(level + 1) * k, :] = moved[k:]


def back_kernel(first, count, u_ref, high_ref, low_ref, ah_ref, al_ref, out_ref):
    n = u_ref.shape[0]
    uh, ul = split(u_ref[...])
    low = low_ref[...]
    left = jnp.concatenate([high_ref[...], uh, ul], axis=0)
    m = low.shape[0]
    ah = jnp.concatenate([ah_ref[first + s] for s in range(count)], axis=1)
    al = jnp.concatenate([al_ref[first + s] for s in range(count)], axis=1)
    one = dot(left, ah)
    three = dot(left[:m + n], al)
    out_ref[:m, :] = one[:m] + dot(low, ah) + three[:m]
    out_ref[m:, :] = one[m:m + n] + one[m + n:] + three[m:]


def tree_kernel(where_ref, inverse_ref, parent_ref, to_root_ref, own_ref, root_ref):
    k = inverse_ref.shape[1]
    near, sibling, middle = where_ref[1], where_ref[2], where_ref[3]
    top = inverse_ref.shape[0] - 1
    inv0, inv1, inv2 = inverse_ref[near], inverse_ref[middle], inverse_ref[top]
    g0 = full(parent_ref[near], inv0)
    gs = full(parent_ref[sibling], inverse_ref[sibling])
    g1 = full(parent_ref[middle], inv1)
    to_root_ref[:, :k] = g1
    to_root_ref[:, k:2 * k] = -full(g1, g0)
    to_root_ref[:, 2 * k:] = -full(g1, gs)
    own_ref[0] = g0
    own_ref[1] = gs
    own_ref[2] = full(inv0, inv0, TN)
    own_ref[3] = full(inv1, inv1, TN)
    h2 = full(inv2, inv2, TN)
    k1 = full(h2, g1)
    root_ref[:, :k] = full(k1, g0)
    root_ref[:, k:2 * k] = -k1
    root_ref[:, 2 * k:] = h2


def join_kernel(mine0_ref, mine1_ref, got0_ref, got1_ref, root_ref, base_ref, low_ref, qh_ref, ql_ref):
    k = root_ref.shape[0]
    root = root_ref[...]
    m = root.shape[1]
    columns = mine0_ref.shape[1]
    for s, (mine, got) in enumerate(((mine0_ref, got0_ref), (mine1_ref, got1_ref))):
        cols = slice(s * columns, (s + 1) * columns)
        b = mine[:m, :] + got[:m, :]
        base_ref[:, cols] = mine[m:, :] + got[m:, :]
        low_ref[:, cols] = b[:2 * k]
        qh, ql = split(product(root, split(b)))
        qh_ref[:, cols] = qh
        ql_ref[:, cols] = ql
    rh, rl = split(root)
    qh_ref[:, 2 * columns:] = rh
    ql_ref[:, 2 * columns:] = rl


def middle_kernel(where_ref, own_ref, other_ref, rhs_ref, to_root_ref, source_ref, up_ref):
    k = to_root_ref.shape[0]
    own = own_ref[...]
    both = own + other_ref[...]
    source = jnp.concatenate(
        [
            rhs_ref[where_ref[3]] - both[:, k:2 * k],
            rhs_ref[where_ref[1]] - own[:, :k],
            rhs_ref[where_ref[2]] - other_ref[:, :k],
        ],
        axis=1,
    )
    source_ref[...] = source
    up_ref[...] = both[:, 2 * k:] + product(source, split(to_root_ref[...]), NT)


def lower_kernel(source_ref, own_ref, base_ref, low_ref, pre_ref, solved_ref):
    k = own_ref.shape[1]
    t1, s0, sb = source_ref[:, :k], source_ref[:, k:2 * k], source_ref[:, 2 * k:]
    c0 = product(s0, split(own_ref[2]))
    s1 = t1 - product(s0, split(own_ref[0]), NT) - product(sb, split(own_ref[1]), NT)
    c1 = product(s1, split(own_ref[3]))
    c0 = c0 - product(c1, split(own_ref[0]))
    solved_ref[0] = c0
    solved_ref[1] = c1
    pre_ref[...] = base_ref[...] - product(jnp.concatenate([c0, c1], axis=1), split(low_ref[...]))


def last_kernel(up_ref, other_ref, rhs_ref, pre_ref, solved_ref, qh_ref, ql_ref, out_ref, sep_ref):
    k = up_ref.shape[1]
    width = pre_ref.shape[1]
    s2 = rhs_ref[rhs_ref.shape[0] - 1] - (up_ref[...] + other_ref[...])
    add = product(s2, (qh_ref[...], ql_ref[...]))
    out_ref[...] = pre_ref[...] - add[:, :width]
    sep_ref[0] = solved_ref[0] + add[:, width:width + k]
    sep_ref[1] = solved_ref[1] + add[:, width + k:width + 2 * k]
    sep_ref[2] = add[:, width + 2 * k:]


def swap_core(x):
    return lax.ppermute(x, "sep", [(0, 1), (1, 0)])


def swap_leaf(x, mask):
    return lax.ppermute(x, "leaf", [(i, i ^ mask) for i in range(lax.axis_size("leaf"))])


def ordered(*arrays):
    return lax.optimization_barrier(arrays)


def local(leaf_rhs, leaf_inverse, skeleton_index, leaf_coupling, sep_rhs, sep_inverse, sep_parent):
    side = lax.axis_index("sep")
    leaf = lax.axis_index("leaf")
    plane = leaf // 32
    where = jnp.stack([side, plane, plane ^ 1, 4 + plane // 2]).astype(jnp.int32)
    mine, index, coupling = leaf_rhs[0], skeleton_index[0], leaf_coupling[0]
    inverse = leaf_inverse[0]
    n, half = mine.shape
    levels, k = index.shape
    m = levels * k
    chunk = 256
    slots = [pltpu.VMEM((half // chunk, half, chunk), F32), pltpu.SemaphoreType.DMA((half // chunk,))]
    steps = half // chunk
    parts = [shape(steps, half, chunk, dtype=BF16)] * 2
    theirs = swap_core(mine)
    part, *home = call("first_half", functools.partial(first_kernel, chunk), [shape(n, half)] + parts,
                       [SMEM, VMEM, HBM], slots, limit=48)(where, mine, inverse)
    term, u, *away = call("second_half", functools.partial(second_kernel, chunk), [shape(n, m), shape(n, half)] + parts,
                          [SMEM, VMEM, VMEM, VMEM, VMEM, HBM], slots, limit=48)(where, theirs, part, index, coupling, inverse)
    term, index, coupling = ordered(term, index, coupling)
    got = swap_core(term)
    high, low = call("spread", spread_kernel, [shape(m, half, dtype=BF16)] * 2, [SMEM, VMEM, VMEM])(where, index, coupling)
    term, high, low, got = ordered(term, high, low, got)
    total = term + got

    def back(first, u, split_inverse):
        out, = call("back", functools.partial(back_kernel, first, steps // 2), [shape(m + n, half // 2)],
                    [VMEM] * 5)(u, high, low, *split_inverse)
        return out

    sent = []
    kept = []
    for mask, first, held in ((1, 0, away), (2, steps // 2, away), (6, 0, home), (8, steps // 2, home)):
        total, u = ordered(total, u)
        got = swap_leaf(total, mask)
        out = back(first, u, held)
        total, out, got = ordered(total, out, got)
        if held is away:
            sent.append(swap_core(out))
        else:
            kept.append(out)
        total = total + got
    total, sep_inverse, sep_parent = ordered(total, sep_inverse, sep_parent)
    got = swap_leaf(total, 24)
    to_root, own, root = call("tree", tree_kernel, [shape(k, m), shape(4, k, k), shape(k, m)],
                              [SMEM, VMEM, VMEM])(where, sep_inverse, sep_parent)
    total, to_root, got = ordered(total, to_root, got)
    total = total + got
    total, root = ordered(total, root)
    got = swap_leaf(total, 32)
    base, lower, qh, ql = call("join", join_kernel,
                               [shape(n, half), shape(2 * k, half)] + [shape(k, half + m, dtype=BF16)] * 2,
                               [VMEM] * 5)(kept[0], kept[1], sent[0], sent[1], root)
    total, got, base = ordered(total, got, base)
    source, up = call("middle", middle_kernel, [shape(n, m), shape(n, k)], [SMEM] + [VMEM] * 4)(
        where, total, got, sep_rhs, to_root)
    other = swap_leaf(up, 96)
    pre, solved = call("lower", lower_kernel, [shape(n, half), shape(2, n, k)], [VMEM] * 4)(source, own, base, lower)
    pre, other = ordered(pre, other)
    out, sep = call("last", last_kernel, [shape(n, half), shape(levels, n, k)], [VMEM] * 7)(
        up, other, sep_rhs, pre, solved, qh, ql)
    return (out[None], sep[None])


def solution(mesh):
    placed = (
        P("leaf", None, "sep"),
        P("leaf", "sep", None),
        P("leaf", None, None),
        P("leaf", None, None, None),
        P(),
        P(),
        P(),
    )
    return jax.shard_map(
        local,
        mesh=mesh,
        in_specs=placed,
        out_specs=(P("leaf", None, "sep"), P("leaf", None, None, None)),
        check_vma=False,
    )
```

```python
import functools

import jax
import jax.numpy as jnp
from jax import lax
from jax.experimental import pallas as pl
from jax.experimental.pallas import tpu as pltpu
from jax.sharding import PartitionSpec as P

F32, BF16 = jnp.float32, jnp.bfloat16
HIGH = lax.Precision.HIGHEST
MIB = 1 << 20
VMEM = pl.BlockSpec(memory_space=pltpu.VMEM)
HBM = pl.BlockSpec(memory_space=pltpu.HBM)
NN = (((1,), (0,)), ((), ()))
NT = (((1,), (1,)), ((), ()))
TN = (((0,), (0,)), ((), ()))


def shape(*dims, dtype=F32):
    return jax.ShapeDtypeStruct(dims, dtype)


def dot(a, b, dims=NN):
    return lax.dot_general(a, b, dims, preferred_element_type=F32)


def full(a, b, dims=NN):
    return lax.dot_general(a, b, dims, precision=HIGH, preferred_element_type=F32)


def split(x):
    high = x.astype(BF16)
    return high, (x - high.astype(F32)).astype(BF16)


def product(a, split_b, dims=NN):
    ah, al = split(a)
    bh, bl = split_b
    rows = a.shape[0]
    both = dot(jnp.concatenate([ah, al], axis=0), bh, dims)
    return both[:rows] + both[rows:] + dot(ah, bl, dims)


def call(name, body, outs, ins, scratch=(), limit=24):
    return pl.pallas_call(
        body,
        out_shape=outs,
        in_specs=ins,
        out_specs=[VMEM] * len(outs),
        scratch_shapes=list(scratch),
        compiler_params=pltpu.CompilerParams(vmem_limit_bytes=limit * MIB),
        name=name,
    )


def load_columns(inverse_ref, first, steps, chunk, a_ref, sems):
    copies = []
    for s in range(steps):
        start = pl.multiple_of(first + s * chunk, chunk)
        copy = pltpu.make_async_copy(inverse_ref.at[:, pl.ds(start, chunk)], a_ref.at[s], sems.at[s])
        copy.start()
        copies.append(copy)
    return copies


def load_kernel(chunk, inverse_ref, ah_ref, al_ref, a_ref, sems):
    steps, half = a_ref.shape[:2]
    copies = load_columns(inverse_ref, lax.axis_index("sep") * half, steps, chunk, a_ref, sems)
    for s, copy in enumerate(copies):
        copy.wait()
        ah_ref[s], al_ref[s] = split(a_ref[s])


def paired(x):
    return jnp.concatenate(split(x), axis=0)


def one_hot(index_ref, level, rows, first):
    row = lax.broadcasted_iota(jnp.int32, (rows, index_ref.shape[1]), 0) + first
    return jnp.where(row == index_ref[level:level + 1, :], 1.0, 0.0).astype(BF16)


def leaf_kernel(chunk, mine_ref, theirs_ref, index_ref, coupling_ref, hh_ref, hl_ref, inverse_ref, term_ref, u_ref, ah_ref, al_ref, a_ref, sems):
    n, half = mine_ref.shape
    levels, k = index_ref.shape
    side = lax.axis_index("sep")
    copies = load_columns(inverse_ref, (1 - side) * half, half // chunk, chunk, a_ref, sems)
    total = jnp.zeros((2 * n, half), F32)
    for s in range(half // chunk):
        x = paired(mine_ref[:, s * chunk:(s + 1) * chunk])
        total = total + (dot(x, hh_ref[s], NT) + dot(x, hl_ref[s], NT))
    hot = [one_hot(index_ref, level, half, side * half) for level in range(levels)]
    for s, copy in enumerate(copies):
        x = paired(theirs_ref[:, s * chunk:(s + 1) * chunk])
        copy.wait()
        ah, al = split(a_ref[s])
        ah_ref[s] = ah
        al_ref[s] = al
        total = total + (dot(x, ah, NT) + dot(x, al, NT))
    u = total[:n] + total[n:]
    u_ref[...] = u
    uh, um = split(u)
    ul = (u - uh.astype(F32) - um.astype(F32)).astype(BF16)
    parts = jnp.concatenate([uh, um, ul], axis=0)
    for level in range(levels):
        picked = dot(parts, hot[level])
        picked = picked[:n] + picked[n:2 * n] + picked[2 * n:]
        term_ref[:, level * k:(level + 1) * k] = product(picked, split(coupling_ref[level]), NT)


def spread_kernel(index_ref, coupling_ref, high_ref, low_ref):
    levels, k = index_ref.shape
    half = high_ref.shape[1]
    for level in range(levels):
        hot = one_hot(index_ref, level, half, lax.axis_index("sep") * half)
        ch, cl = split(coupling_ref[level])
        moved = dot(jnp.concatenate([ch, cl], axis=0), hot, NT).astype(BF16)
        high_ref[level * k:(level + 1) * k, :] = moved[:k]
        low_ref[level * k:(level + 1) * k, :] = moved[k:]


def back_kernel(first, count, u_ref, high_ref, low_ref, ah_ref, al_ref, out_ref):
    n = u_ref.shape[0]
    uh, ul = split(u_ref[...])
    low = low_ref[...]
    left = jnp.concatenate([high_ref[...], uh, ul], axis=0)
    m = low.shape[0]
    ah = jnp.concatenate([ah_ref[first + s] for s in range(count)], axis=1)
    al = jnp.concatenate([al_ref[first + s] for s in range(count)], axis=1)
    one = dot(left, ah)
    three = dot(left[:m + n], al)
    out_ref[:m, :] = one[:m] + dot(low, ah) + three[:m]
    out_ref[m:, :] = one[m:m + n] + one[m + n:] + three[m:]


def pair_matrices(inverse_ref, parent_ref, near, sibling, middle):
    g0 = full(parent_ref[near], inverse_ref[near])
    gs = full(parent_ref[sibling], inverse_ref[sibling])
    g1 = full(parent_ref[middle], inverse_ref[middle])
    return g0, gs, g1, jnp.concatenate([g1, -full(g1, g0), -full(g1, gs)], axis=1)


def tree_kernel(inverse_ref, parent_ref, rhs_ref, wayh_ref, wayl_ref, own_ref, root_ref, chosen_ref):
    k = inverse_ref.shape[1]
    plane = lax.axis_index("leaf") >> 5
    near, sibling, middle = plane, plane ^ 1, 4 + (plane >> 1)
    top = inverse_ref.shape[0] - 1
    inv0, inv1, inv2 = inverse_ref[near], inverse_ref[middle], inverse_ref[top]
    g0, gs, g1, way = pair_matrices(inverse_ref, parent_ref, near, sibling, middle)
    wayh_ref[0], wayl_ref[0] = split(way)
    way = pair_matrices(inverse_ref, parent_ref, 3 - near, (3 - near) ^ 1, 9 - middle)[3]
    wayh_ref[1], wayl_ref[1] = split(way)
    own_ref[0] = g0
    own_ref[1] = gs
    own_ref[2] = full(inv0, inv0, TN)
    own_ref[3] = full(inv1, inv1, TN)
    h2 = full(inv2, inv2, TN)
    k1 = full(h2, g1)
    root_ref[:, :k] = full(k1, g0)
    root_ref[:, k:2 * k] = -k1
    root_ref[:, 2 * k:] = h2
    chosen_ref[:, :k] = rhs_ref[middle]
    chosen_ref[:, k:2 * k] = rhs_ref[near]
    chosen_ref[:, 2 * k:3 * k] = rhs_ref[sibling]
    chosen_ref[:, 3 * k:] = rhs_ref[top]


def join_kernel(mine0_ref, mine1_ref, got0_ref, got1_ref, root_ref, base_ref, low_ref, qh_ref, ql_ref):
    k = root_ref.shape[0]
    root = root_ref[...]
    m = root.shape[1]
    columns = mine0_ref.shape[1]
    for s, (mine, got) in enumerate(((mine0_ref, got0_ref), (mine1_ref, got1_ref))):
        cols = slice(s * columns, (s + 1) * columns)
        b = mine[:m, :] + got[:m, :]
        base_ref[:, cols] = mine[m:, :] + got[m:, :]
        low_ref[:, cols] = b[:2 * k]
        qh, ql = split(product(root, split(b)))
        qh_ref[:, cols] = qh
        ql_ref[:, cols] = ql
    rh, rl = split(root)
    qh_ref[:, 2 * columns:] = rh
    ql_ref[:, 2 * columns:] = rl


def source_kernel(own_ref, other_ref, chosen_ref, out_ref):
    k = own_ref.shape[1] // 3
    out_ref[:, :k] = chosen_ref[:, :k] - own_ref[:, k:2 * k] - other_ref[:, k:2 * k]
    out_ref[:, k:2 * k] = chosen_ref[:, k:2 * k] - own_ref[:, :k]
    out_ref[:, 2 * k:3 * k] = chosen_ref[:, 2 * k:3 * k] - other_ref[:, :k]
    out_ref[:, 3 * k:] = own_ref[:, 2 * k:] + other_ref[:, 2 * k:]


def lower_kernel(source_ref, chosen_ref, wayh_ref, wayl_ref, own_ref, base_ref, low_ref, pre_ref, solved_ref, top_ref):
    k = own_ref.shape[1]
    t1, s0, sb = source_ref[:, :k], source_ref[:, k:2 * k], source_ref[:, 2 * k:3 * k]
    c0 = product(s0, split(own_ref[2]))
    s1 = t1 - product(s0, split(own_ref[0]), NT) - product(sb, split(own_ref[1]), NT)
    c1 = product(s1, split(own_ref[3]))
    c0 = c0 - product(c1, split(own_ref[0]))
    solved_ref[0] = c0
    solved_ref[1] = c1
    pre_ref[...] = base_ref[...] - product(jnp.concatenate([c0, c1], axis=1), split(low_ref[...]))
    up = product(source_ref[:, :3 * k], (wayh_ref[0], wayl_ref[0]), NT)
    top_ref[...] = chosen_ref[:, 3 * k:] - source_ref[:, 3 * k:] - up


def last_kernel(other_ref, wayh_ref, wayl_ref, top_ref, pre_ref, solved_ref, qh_ref, ql_ref, out_ref, sep_ref):
    k = top_ref.shape[1]
    width = pre_ref.shape[1]
    up = product(other_ref[:, :3 * k], (wayh_ref[1], wayl_ref[1]), NT)
    s2 = top_ref[...] - other_ref[:, 3 * k:] - up
    add = product(s2, (qh_ref[...], ql_ref[...]))
    out_ref[...] = pre_ref[...] - add[:, :width]
    sep_ref[0] = solved_ref[0] + add[:, width:width + k]
    sep_ref[1] = solved_ref[1] + add[:, width + k:width + 2 * k]
    sep_ref[2] = add[:, width + 2 * k:]


def swap_core(x):
    return lax.ppermute(x, "sep", [(0, 1), (1, 0)])


def swap_leaf(x, mask):
    return lax.ppermute(x, "leaf", [(i, i ^ mask) for i in range(lax.axis_size("leaf"))])


def ordered(*arrays):
    return lax.optimization_barrier(arrays)


def local(leaf_rhs, leaf_inverse, skeleton_index, leaf_coupling, sep_rhs, sep_inverse, sep_parent):
    mine, index, coupling = leaf_rhs[0], skeleton_index[0], leaf_coupling[0]
    inverse = leaf_inverse[0]
    n, half = mine.shape
    levels, k = index.shape
    m = levels * k
    chunk = 256
    steps = half // chunk
    slots = [pltpu.VMEM((steps, half, chunk), F32), pltpu.SemaphoreType.DMA((steps,))]
    parts = [shape(steps, half, chunk, dtype=BF16)] * 2
    theirs = swap_core(mine)
    home = call("load", functools.partial(load_kernel, chunk), parts, [HBM], slots, limit=48)(inverse)
    term, u, *away = call("leaf", functools.partial(leaf_kernel, chunk), [shape(n, m), shape(n, half)] + parts,
                          [VMEM] * 6 + [HBM], slots, limit=43)(mine, theirs, index, coupling, *home, inverse)
    term, index, coupling = ordered(term, index, coupling)
    got = swap_core(term)
    high, low = call("spread", spread_kernel, [shape(m, half, dtype=BF16)] * 2, [VMEM, VMEM])(index, coupling)
    term, high, low, got = ordered(term, high, low, got)
    total = term + got

    def back(first, u, split_inverse):
        out, = call("back", functools.partial(back_kernel, first, steps // 2), [shape(m + n, half // 2)],
                    [VMEM] * 5)(u, high, low, *split_inverse)
        return out

    sent = []
    kept = []
    for mask, first, held in ((1, 0, away), (3, steps // 2, away), (6, 0, home), (8, steps // 2, home)):
        total, u = ordered(total, u)
        got = swap_leaf(total, mask)
        out = back(first, u, held)
        if held is away:
            sent.append(swap_core(out))
        else:
            kept.append(out)
        total, out, got = ordered(total, out, got)
        total = total + got
    total, sep_inverse, sep_parent = ordered(total, sep_inverse, sep_parent)
    got = swap_leaf(total, 24)
    wayh, wayl, own, root, chosen = call(
        "tree", tree_kernel,
        [shape(2, k, m, dtype=BF16)] * 2 + [shape(4, k, k), shape(k, m), shape(n, m + k)],
        [VMEM] * 3)(sep_inverse, sep_parent, sep_rhs)
    total, root, got = ordered(total, root, got)
    total = total + got
    total, root = ordered(total, root)
    got = swap_leaf(total, 32)
    base, lower, qh, ql = call("join", join_kernel,
                               [shape(n, half), shape(2 * k, half)] + [shape(k, half + m, dtype=BF16)] * 2,
                               [VMEM] * 5)(kept[0], kept[1], sent[0], sent[1], root)
    total, got, base = ordered(total, got, base)
    source, = call("source", source_kernel, [shape(n, m + k)], [VMEM] * 3)(total, got, chosen)
    other = swap_leaf(source, 96)
    pre, solved, top = call("lower", lower_kernel, [shape(n, half), shape(2, n, k), shape(n, k)], [VMEM] * 7)(
        source, chosen, wayh, wayl, own, base, lower)
    pre, other = ordered(pre, other)
    out, sep = call("last", last_kernel, [shape(n, half), shape(levels, n, k)], [VMEM] * 8)(
        other, wayh, wayl, top, pre, solved, qh, ql)
    return (out[None], sep[None])


def solution(mesh):
    placed = (
        P("leaf", None, "sep"),
        P("leaf", "sep", None),
        P("leaf", None, None),
        P("leaf", None, None, None),
        P(),
        P(),
        P(),
    )
    return jax.shard_map(
        local,
        mesh=mesh,
        in_specs=placed,
        out_specs=(P("leaf", None, "sep"), P("leaf", None, None, None)),
        check_vma=False,
    )
```

```python
import functools

import jax
import jax.numpy as jnp
from jax import lax
from jax.experimental import pallas as pl
from jax.experimental.pallas import tpu as pltpu
from jax.sharding import PartitionSpec as P

F32, BF16 = jnp.float32, jnp.bfloat16
HIGH = lax.Precision.HIGHEST
MIB = 1 << 20
VMEM = pl.BlockSpec(memory_space=pltpu.VMEM)
HBM = pl.BlockSpec(memory_space=pltpu.HBM)
NN = (((1,), (0,)), ((), ()))
NT = (((1,), (1,)), ((), ()))
TN = (((0,), (0,)), ((), ()))


def shape(*dims, dtype=F32):
    return jax.ShapeDtypeStruct(dims, dtype)


def dot(a, b, dims=NN):
    return lax.dot_general(a, b, dims, preferred_element_type=F32)


def full(a, b, dims=NN):
    return lax.dot_general(a, b, dims, precision=HIGH, preferred_element_type=F32)


def split(x):
    high = x.astype(BF16)
    return high, (x - high.astype(F32)).astype(BF16)


def product(a, split_b, dims=NN):
    ah, al = split(a)
    bh, bl = split_b
    rows = a.shape[0]
    both = dot(jnp.concatenate([ah, al], axis=0), bh, dims)
    return both[:rows] + both[rows:] + dot(ah, bl, dims)


def call(name, body, outs, ins, scratch=(), limit=24):
    return pl.pallas_call(
        body,
        out_shape=outs,
        in_specs=ins,
        out_specs=[VMEM] * len(outs),
        scratch_shapes=list(scratch),
        compiler_params=pltpu.CompilerParams(vmem_limit_bytes=limit * MIB),
        name=name,
    )


def load_columns(inverse_ref, first, steps, chunk, a_ref, sems):
    copies = []
    for s in range(steps):
        start = pl.multiple_of(first + s * chunk, chunk)
        copy = pltpu.make_async_copy(inverse_ref.at[:, pl.ds(start, chunk)], a_ref.at[s], sems.at[s])
        copy.start()
        copies.append(copy)
    return copies


def load_kernel(chunk, inverse_ref, ah_ref, al_ref, a_ref, sems):
    steps, half = a_ref.shape[:2]
    copies = load_columns(inverse_ref, lax.axis_index("sep") * half, steps, chunk, a_ref, sems)
    for s, copy in enumerate(copies):
        copy.wait()
        ah_ref[s], al_ref[s] = split(a_ref[s])


def paired(x):
    return jnp.concatenate(split(x), axis=0)


def one_hot(index_ref, level, rows, first):
    row = lax.broadcasted_iota(jnp.int32, (rows, index_ref.shape[2]), 0) + first
    return jnp.where(row == index_ref[level], 1.0, 0.0).astype(BF16)


def leaf_kernel(chunk, mine_ref, theirs_ref, index_ref, coupling_ref, hh_ref, hl_ref, inverse_ref, term_ref, u_ref, ah_ref, al_ref, a_ref, sems):
    n, half = mine_ref.shape
    levels, _, k = index_ref.shape
    side = lax.axis_index("sep")
    copies = load_columns(inverse_ref, (1 - side) * half, half // chunk, chunk, a_ref, sems)
    total = jnp.zeros((2 * n, half), F32)
    for s in range(half // chunk):
        x = paired(mine_ref[:, s * chunk:(s + 1) * chunk])
        total = total + (dot(x, hh_ref[s], NT) + dot(x, hl_ref[s], NT))
    hot = [one_hot(index_ref, level, half, side * half) for level in range(levels)]
    for s, copy in enumerate(copies):
        x = paired(theirs_ref[:, s * chunk:(s + 1) * chunk])
        copy.wait()
        ah, al = split(a_ref[s])
        ah_ref[s] = ah
        al_ref[s] = al
        total = total + (dot(x, ah, NT) + dot(x, al, NT))
    u = total[:n] + total[n:]
    u_ref[...] = u
    uh, um = split(u)
    ul = (u - uh.astype(F32) - um.astype(F32)).astype(BF16)
    parts = jnp.concatenate([uh, um, ul], axis=0)
    for level in range(levels):
        picked = dot(parts, hot[level])
        picked = picked[:n] + picked[n:2 * n] + picked[2 * n:]
        term_ref[:, level * k:(level + 1) * k] = product(picked, split(coupling_ref[level]), NT)


def spread_kernel(index_ref, coupling_ref, high_ref, low_ref):
    levels, _, k = index_ref.shape
    half = high_ref.shape[1]
    for level in range(levels):
        hot = one_hot(index_ref, level, half, lax.axis_index("sep") * half)
        ch, cl = split(coupling_ref[level])
        moved = dot(jnp.concatenate([ch, cl], axis=0), hot, NT).astype(BF16)
        high_ref[level * k:(level + 1) * k, :] = moved[:k]
        low_ref[level * k:(level + 1) * k, :] = moved[k:]


def back_kernel(first, count, u_ref, high_ref, low_ref, ah_ref, al_ref, out_ref):
    n = u_ref.shape[0]
    uh, ul = split(u_ref[...])
    low = low_ref[...]
    left = jnp.concatenate([high_ref[...], uh, ul], axis=0)
    m = low.shape[0]
    ah = jnp.concatenate([ah_ref[first + s] for s in range(count)], axis=1)
    al = jnp.concatenate([al_ref[first + s] for s in range(count)], axis=1)
    one = dot(left, ah)
    three = dot(left[:m + n], al)
    out_ref[:m, :] = one[:m] + dot(low, ah) + three[:m]
    out_ref[m:, :] = one[m:m + n] + one[m + n:] + three[m:]


def pair_matrices(inverse_ref, parent_ref, near, sibling, middle):
    g0 = full(parent_ref[near], inverse_ref[near])
    gs = full(parent_ref[sibling], inverse_ref[sibling])
    g1 = full(parent_ref[middle], inverse_ref[middle])
    return g0, gs, g1, jnp.concatenate([g1, -full(g1, g0), -full(g1, gs)], axis=1)


def tree_kernel(inverse_ref, parent_ref, rhs_ref, wayh_ref, wayl_ref, own_ref, root_ref, chosen_ref):
    k = inverse_ref.shape[1]
    plane = lax.axis_index("leaf") >> 5
    near, sibling, middle = plane, plane ^ 1, 4 + (plane >> 1)
    top = inverse_ref.shape[0] - 1
    inv0, inv1, inv2 = inverse_ref[near], inverse_ref[middle], inverse_ref[top]
    g0, gs, g1, way = pair_matrices(inverse_ref, parent_ref, near, sibling, middle)
    wayh_ref[0], wayl_ref[0] = split(way)
    way = pair_matrices(inverse_ref, parent_ref, 3 - near, (3 - near) ^ 1, 9 - middle)[3]
    wayh_ref[1], wayl_ref[1] = split(way)
    own_ref[0] = g0
    own_ref[1] = gs
    own_ref[2] = full(inv0, inv0, TN)
    own_ref[3] = full(inv1, inv1, TN)
    h2 = full(inv2, inv2, TN)
    k1 = full(h2, g1)
    root_ref[:, :k] = full(k1, g0)
    root_ref[:, k:2 * k] = -k1
    root_ref[:, 2 * k:] = h2
    chosen_ref[:, :k] = rhs_ref[middle]
    chosen_ref[:, k:2 * k] = rhs_ref[near]
    chosen_ref[:, 2 * k:3 * k] = rhs_ref[sibling]
    chosen_ref[:, 3 * k:] = rhs_ref[top]


def join_kernel(mine0_ref, mine1_ref, got0_ref, got1_ref, root_ref, base_ref, low_ref, qh_ref, ql_ref):
    k = root_ref.shape[0]
    root = root_ref[...]
    m = root.shape[1]
    columns = mine0_ref.shape[1]
    for s, (mine, got) in enumerate(((mine0_ref, got0_ref), (mine1_ref, got1_ref))):
        cols = slice(s * columns, (s + 1) * columns)
        b = mine[:m, :] + got[:m, :]
        base_ref[:, cols] = mine[m:, :] + got[m:, :]
        low_ref[:, cols] = b[:2 * k]
        qh, ql = split(product(root, split(b)))
        qh_ref[:, cols] = qh
        ql_ref[:, cols] = ql
    rh, rl = split(root)
    qh_ref[:, 2 * columns:] = rh
    ql_ref[:, 2 * columns:] = rl


def source_kernel(own_ref, other_ref, chosen_ref, out_ref):
    k = own_ref.shape[1] // 3
    out_ref[:, :k] = chosen_ref[:, :k] - own_ref[:, k:2 * k] - other_ref[:, k:2 * k]
    out_ref[:, k:2 * k] = chosen_ref[:, k:2 * k] - own_ref[:, :k]
    out_ref[:, 2 * k:3 * k] = chosen_ref[:, 2 * k:3 * k] - other_ref[:, :k]
    out_ref[:, 3 * k:] = own_ref[:, 2 * k:] + other_ref[:, 2 * k:]


def lower_kernel(source_ref, chosen_ref, wayh_ref, wayl_ref, own_ref, base_ref, low_ref, pre_ref, solved_ref, top_ref):
    k = own_ref.shape[1]
    t1, s0, sb = source_ref[:, :k], source_ref[:, k:2 * k], source_ref[:, 2 * k:3 * k]
    c0 = product(s0, split(own_ref[2]))
    s1 = t1 - product(s0, split(own_ref[0]), NT) - product(sb, split(own_ref[1]), NT)
    c1 = product(s1, split(own_ref[3]))
    c0 = c0 - product(c1, split(own_ref[0]))
    solved_ref[0] = c0
    solved_ref[1] = c1
    pre_ref[...] = base_ref[...] - product(jnp.concatenate([c0, c1], axis=1), split(low_ref[...]))
    up = product(source_ref[:, :3 * k], (wayh_ref[0], wayl_ref[0]), NT)
    top_ref[...] = chosen_ref[:, 3 * k:] - source_ref[:, 3 * k:] - up


def last_kernel(other_ref, wayh_ref, wayl_ref, top_ref, pre_ref, solved_ref, qh_ref, ql_ref, out_ref, sep_ref):
    k = top_ref.shape[1]
    width = pre_ref.shape[1]
    up = product(other_ref[:, :3 * k], (wayh_ref[1], wayl_ref[1]), NT)
    s2 = top_ref[...] - other_ref[:, 3 * k:] - up
    add = product(s2, (qh_ref[...], ql_ref[...]))
    out_ref[...] = pre_ref[...] - add[:, :width]
    sep_ref[0] = solved_ref[0] + add[:, width:width + k]
    sep_ref[1] = solved_ref[1] + add[:, width + k:width + 2 * k]
    sep_ref[2] = add[:, width + 2 * k:]


def swap_core(x):
    return lax.ppermute(x, "sep", [(0, 1), (1, 0)])


def swap_leaf(x, mask):
    count = lax.axis_size("leaf")
    return lax.ppermute(x, ("leaf", "sep"), [(2 * i + 1, 2 * (i ^ mask) + 1) for i in range(count)])


def second_core(x):
    return jnp.where(lax.axis_index("sep") == 1, x, lax.ppermute(x, "sep", [(1, 0)]))


def ordered(*arrays):
    return lax.optimization_barrier(arrays)


def local(leaf_rhs, leaf_inverse, skeleton_index, leaf_coupling, sep_rhs, sep_inverse, sep_parent):
    mine, coupling = leaf_rhs[0], leaf_coupling[0]
    index = jnp.transpose(skeleton_index, (1, 0, 2))
    inverse = leaf_inverse[0]
    n, half = mine.shape
    levels, _, k = index.shape
    m = levels * k
    chunk = 256
    steps = half // chunk
    slots = [pltpu.VMEM((steps, half, chunk), F32), pltpu.SemaphoreType.DMA((steps,))]
    parts = [shape(steps, half, chunk, dtype=BF16)] * 2
    theirs = swap_core(mine)
    home = call("load", functools.partial(load_kernel, chunk), parts, [HBM], slots, limit=48)(inverse)
    term, u, *away = call("leaf", functools.partial(leaf_kernel, chunk), [shape(n, m), shape(n, half)] + parts,
                          [VMEM] * 6 + [HBM], slots, limit=43)(mine, theirs, index, coupling, *home, inverse)
    term, index, coupling = ordered(term, index, coupling)
    got = swap_core(term)
    high, low = call("spread", spread_kernel, [shape(m, half, dtype=BF16)] * 2, [VMEM, VMEM])(index, coupling)
    term, high, low, got = ordered(term, high, low, got)
    total = term + got

    def back(first, u, split_inverse):
        out, = call("back", functools.partial(back_kernel, first, steps // 2), [shape(m + n, half // 2)],
                    [VMEM] * 5)(u, high, low, *split_inverse)
        return out

    made = []
    for mask, first, held in ((1, 0, away), (3, steps // 2, away), (6, 0, home), (8, steps // 2, home)):
        total, u = ordered(total, u)
        got = swap_leaf(total, mask)
        out = back(first, u, held)
        total, out, got = ordered(total, out, got)
        made.append(swap_core(out) if held is away else out)
        total = total + got
    total, sep_inverse, sep_parent = ordered(total, sep_inverse, sep_parent)
    got = swap_leaf(total, 24)
    wayh, wayl, own, root, chosen = call(
        "tree", tree_kernel,
        [shape(2, k, m, dtype=BF16)] * 2 + [shape(4, k, k), shape(k, m), shape(n, m + k)],
        [VMEM] * 3)(sep_inverse, sep_parent, sep_rhs)
    total, root, got = ordered(total, root, got)
    total = total + got
    total, root = ordered(total, root)
    got = swap_leaf(total, 32)
    base, lower, qh, ql = call("join", join_kernel,
                               [shape(n, half), shape(2 * k, half)] + [shape(k, half + m, dtype=BF16)] * 2,
                               [VMEM] * 5)(made[2], made[3], made[0], made[1], root)
    total, got, base = ordered(total, got, base)
    source, = call("source", source_kernel, [shape(n, m + k)], [VMEM] * 3)(total, got, chosen)
    other = swap_leaf(source, 96)
    source = second_core(source)
    pre, solved, top = call("lower", lower_kernel, [shape(n, half), shape(2, n, k), shape(n, k)], [VMEM] * 7)(
        source, chosen, wayh, wayl, own, base, lower)
    pre, other = ordered(pre, other)
    other = second_core(other)
    out, sep = call("last", last_kernel, [shape(n, half), shape(levels, n, k)], [VMEM] * 8)(
        other, wayh, wayl, top, pre, solved, qh, ql)
    return (out[None], sep[None])


def solution(mesh):
    placed = (
        P("leaf", None, "sep"),
        P("leaf", "sep", None),
        P("leaf", None, None),
        P("leaf", None, None, None),
        P(),
        P(),
        P(),
    )
    return jax.shard_map(
        local,
        mesh=mesh,
        in_specs=placed,
        out_specs=(P("leaf", None, "sep"), P("leaf", None, None, None)),
        check_vma=False,
    )
```

```python
import functools

import jax
import jax.numpy as jnp
from jax import lax
from jax.experimental import pallas as pl
from jax.experimental.pallas import tpu as pltpu
from jax.sharding import PartitionSpec as P

F32, BF16 = jnp.float32, jnp.bfloat16
HIGH = lax.Precision.HIGHEST
MIB = 1 << 20
VMEM = pl.BlockSpec(memory_space=pltpu.VMEM)
HBM = pl.BlockSpec(memory_space=pltpu.HBM)
NN = (((1,), (0,)), ((), ()))
NT = (((1,), (1,)), ((), ()))
TN = (((0,), (0,)), ((), ()))


def shape(*dims, dtype=F32):
    return jax.ShapeDtypeStruct(dims, dtype)


def dot(a, b, dims=NN):
    return lax.dot_general(a, b, dims, preferred_element_type=F32)


def full(a, b, dims=NN):
    return lax.dot_general(a, b, dims, precision=HIGH, preferred_element_type=F32)


def split(x):
    high = x.astype(BF16)
    return high, (x - high.astype(F32)).astype(BF16)


def product(a, split_b, dims=NN):
    ah, al = split(a)
    bh, bl = split_b
    rows = a.shape[0]
    both = dot(jnp.concatenate([ah, al], axis=0), bh, dims)
    return both[:rows] + both[rows:] + dot(ah, bl, dims)


def call(name, body, outs, ins, scratch=(), limit=24):
    return pl.pallas_call(
        body,
        out_shape=outs,
        in_specs=ins,
        out_specs=[VMEM] * len(outs),
        scratch_shapes=list(scratch),
        compiler_params=pltpu.CompilerParams(vmem_limit_bytes=limit * MIB),
        name=name,
    )


def load_columns(inverse_ref, first, steps, chunk, a_ref, sems):
    copies = []
    for s in range(steps):
        start = pl.multiple_of(first + s * chunk, chunk)
        copy = pltpu.make_async_copy(inverse_ref.at[:, pl.ds(start, chunk)], a_ref.at[s], sems.at[s])
        copy.start()
        copies.append(copy)
    return copies


def load_kernel(chunk, inverse_ref, ah_ref, al_ref, a_ref, sems):
    steps, half = a_ref.shape[:2]
    copies = load_columns(inverse_ref, lax.axis_index("sep") * half, steps, chunk, a_ref, sems)
    for s, copy in enumerate(copies):
        copy.wait()
        ah_ref[s], al_ref[s] = split(a_ref[s])


def paired(x):
    return jnp.concatenate(split(x), axis=0)


def one_hot(index_ref, level, rows, first):
    row = lax.broadcasted_iota(jnp.int32, (rows, index_ref.shape[2]), 0) + first
    return jnp.where(row == index_ref[level], 1.0, 0.0).astype(BF16)


def leaf_kernel(chunk, mine_ref, theirs_ref, index_ref, coupling_ref, hh_ref, hl_ref, inverse_ref, term_ref, u_ref, ah_ref, al_ref, a_ref, sems):
    n, half = mine_ref.shape
    levels, _, k = index_ref.shape
    side = lax.axis_index("sep")
    copies = load_columns(inverse_ref, (1 - side) * half, half // chunk, chunk, a_ref, sems)
    total = jnp.zeros((2 * n, half), F32)
    for s in range(half // chunk):
        x = paired(mine_ref[:, s * chunk:(s + 1) * chunk])
        total = total + (dot(x, hh_ref[s], NT) + dot(x, hl_ref[s], NT))
    hot = [one_hot(index_ref, level, half, side * half) for level in range(levels)]
    for s, copy in enumerate(copies):
        x = paired(theirs_ref[:, s * chunk:(s + 1) * chunk])
        copy.wait()
        ah, al = split(a_ref[s])
        ah_ref[s] = ah
        al_ref[s] = al
        total = total + (dot(x, ah, NT) + dot(x, al, NT))
    u = total[:n] + total[n:]
    u_ref[...] = u
    uh, um = split(u)
    ul = (u - uh.astype(F32) - um.astype(F32)).astype(BF16)
    parts = jnp.concatenate([uh, um, ul], axis=0)
    for level in range(levels):
        picked = dot(parts, hot[level])
        picked = picked[:n] + picked[n:2 * n] + picked[2 * n:]
        term_ref[:, level * k:(level + 1) * k] = product(picked, split(coupling_ref[level]), NT)


def spread_kernel(index_ref, coupling_ref, high_ref, low_ref):
    levels, _, k = index_ref.shape
    half = high_ref.shape[1]
    for level in range(levels):
        hot = one_hot(index_ref, level, half, lax.axis_index("sep") * half)
        ch, cl = split(coupling_ref[level])
        moved = dot(jnp.concatenate([ch, cl], axis=0), hot, NT).astype(BF16)
        high_ref[level * k:(level + 1) * k, :] = moved[:k]
        low_ref[level * k:(level + 1) * k, :] = moved[k:]


def back_kernel(first, count, u_ref, high_ref, low_ref, ah_ref, al_ref, out_ref):
    n = u_ref.shape[0]
    uh, ul = split(u_ref[...])
    low = low_ref[...]
    left = jnp.concatenate([high_ref[...], uh, ul], axis=0)
    m = low.shape[0]
    ah = jnp.concatenate([ah_ref[first + s] for s in range(count)], axis=1)
    al = jnp.concatenate([al_ref[first + s] for s in range(count)], axis=1)
    one = dot(left, ah)
    three = dot(left[:m + n], al)
    out_ref[:m, :] = one[:m] + dot(low, ah) + three[:m]
    out_ref[m:, :] = one[m:m + n] + one[m + n:] + three[m:]


def pair_matrices(inverse_ref, parent_ref, near, sibling, middle):
    g0 = full(parent_ref[near], inverse_ref[near])
    gs = full(parent_ref[sibling], inverse_ref[sibling])
    g1 = full(parent_ref[middle], inverse_ref[middle])
    return g0, gs, g1, jnp.concatenate([g1, -full(g1, g0), -full(g1, gs)], axis=1)


def tree_kernel(inverse_ref, parent_ref, rhs_ref, wayh_ref, wayl_ref, own_ref, root_ref, chosen_ref):
    k = inverse_ref.shape[1]
    plane = lax.axis_index("leaf") >> 5
    near, sibling, middle = plane, plane ^ 1, 4 + (plane >> 1)
    top = inverse_ref.shape[0] - 1
    inv0, inv1, inv2 = inverse_ref[near], inverse_ref[middle], inverse_ref[top]
    g0, gs, g1, way = pair_matrices(inverse_ref, parent_ref, near, sibling, middle)
    wayh_ref[0], wayl_ref[0] = split(way)
    way = pair_matrices(inverse_ref, parent_ref, 3 - near, (3 - near) ^ 1, 9 - middle)[3]
    wayh_ref[1], wayl_ref[1] = split(way)
    own_ref[0] = g0
    own_ref[1] = gs
    own_ref[2] = full(inv0, inv0, TN)
    own_ref[3] = full(inv1, inv1, TN)
    h2 = full(inv2, inv2, TN)
    k1 = full(h2, g1)
    root_ref[:, :k] = full(k1, g0)
    root_ref[:, k:2 * k] = -k1
    root_ref[:, 2 * k:] = h2
    chosen_ref[:, :k] = rhs_ref[middle]
    chosen_ref[:, k:2 * k] = rhs_ref[near]
    chosen_ref[:, 2 * k:3 * k] = rhs_ref[sibling]
    chosen_ref[:, 3 * k:] = rhs_ref[top]


def join_kernel(mine0_ref, mine1_ref, got0_ref, got1_ref, root_ref, base_ref, low_ref, qh_ref, ql_ref):
    k = root_ref.shape[0]
    root = root_ref[...]
    m = root.shape[1]
    columns = mine0_ref.shape[1]
    for s, (mine, got) in enumerate(((mine0_ref, got0_ref), (mine1_ref, got1_ref))):
        cols = slice(s * columns, (s + 1) * columns)
        b = mine[:m, :] + got[:m, :]
        base_ref[:, cols] = mine[m:, :] + got[m:, :]
        low_ref[:, cols] = b[:2 * k]
        qh, ql = split(product(root, split(b)))
        qh_ref[:, cols] = qh
        ql_ref[:, cols] = ql
    rh, rl = split(root)
    qh_ref[:, 2 * columns:] = rh
    ql_ref[:, 2 * columns:] = rl


def mix_kernel(total_ref, one_ref, two_ref, out_ref):
    first = lax.axis_index("sep") == 0
    out_ref[...] = one_ref[...] + jnp.where(first, total_ref[...], two_ref[...])


def source_kernel(own_ref, other_ref, chosen_ref, out_ref):
    k = own_ref.shape[1] // 3
    out_ref[:, :k] = chosen_ref[:, :k] - own_ref[:, k:2 * k] - other_ref[:, k:2 * k]
    out_ref[:, k:2 * k] = chosen_ref[:, k:2 * k] - own_ref[:, :k]
    out_ref[:, 2 * k:3 * k] = chosen_ref[:, 2 * k:3 * k] - other_ref[:, :k]
    out_ref[:, 3 * k:] = own_ref[:, 2 * k:] + other_ref[:, 2 * k:]


def lower_kernel(source_ref, chosen_ref, wayh_ref, wayl_ref, own_ref, base_ref, low_ref, pre_ref, solved_ref, top_ref):
    k = own_ref.shape[1]
    t1, s0, sb = source_ref[:, :k], source_ref[:, k:2 * k], source_ref[:, 2 * k:3 * k]
    c0 = product(s0, split(own_ref[2]))
    s1 = t1 - product(s0, split(own_ref[0]), NT) - product(sb, split(own_ref[1]), NT)
    c1 = product(s1, split(own_ref[3]))
    c0 = c0 - product(c1, split(own_ref[0]))
    solved_ref[0] = c0
    solved_ref[1] = c1
    pre_ref[...] = base_ref[...] - product(jnp.concatenate([c0, c1], axis=1), split(low_ref[...]))
    up = product(source_ref[:, :3 * k], (wayh_ref[0], wayl_ref[0]), NT)
    top_ref[...] = chosen_ref[:, 3 * k:] - source_ref[:, 3 * k:] - up


def last_kernel(other_ref, wayh_ref, wayl_ref, top_ref, pre_ref, solved_ref, qh_ref, ql_ref, out_ref, sep_ref):
    k = top_ref.shape[1]
    width = pre_ref.shape[1]
    up = product(other_ref[:, :3 * k], (wayh_ref[1], wayl_ref[1]), NT)
    s2 = top_ref[...] - other_ref[:, 3 * k:] - up
    add = product(s2, (qh_ref[...], ql_ref[...]))
    out_ref[...] = pre_ref[...] - add[:, :width]
    sep_ref[0] = solved_ref[0] + add[:, width:width + k]
    sep_ref[1] = solved_ref[1] + add[:, width + k:width + 2 * k]
    sep_ref[2] = add[:, width + 2 * k:]


def swap_core(x):
    return lax.ppermute(x, "sep", [(0, 1), (1, 0)])


def swap_leaf(x, mask, first_mask=None):
    masks = (mask if first_mask is None else first_mask, mask)
    count = 2 * lax.axis_size("leaf")
    return lax.ppermute(x, ("leaf", "sep"), [(i, i ^ 2 * masks[i % 2]) for i in range(count)])


def ordered(*arrays):
    return lax.optimization_barrier(arrays)


def local(leaf_rhs, leaf_inverse, skeleton_index, leaf_coupling, sep_rhs, sep_inverse, sep_parent):
    mine, coupling = leaf_rhs[0], leaf_coupling[0]
    index = jnp.transpose(skeleton_index, (1, 0, 2))
    inverse = leaf_inverse[0]
    n, half = mine.shape
    levels, _, k = index.shape
    m = levels * k
    chunk = 256
    steps = half // chunk
    slots = [pltpu.VMEM((steps, half, chunk), F32), pltpu.SemaphoreType.DMA((steps,))]
    parts = [shape(steps, half, chunk, dtype=BF16)] * 2
    theirs = swap_core(mine)
    home = call("load", functools.partial(load_kernel, chunk), parts, [HBM], slots, limit=48)(inverse)
    term, u, *away = call("leaf", functools.partial(leaf_kernel, chunk), [shape(n, m), shape(n, half)] + parts,
                          [VMEM] * 6 + [HBM], slots, limit=43)(mine, theirs, index, coupling, *home, inverse)
    term, index, coupling = ordered(term, index, coupling)
    got = swap_core(term)
    high, low = call("spread", spread_kernel, [shape(m, half, dtype=BF16)] * 2, [VMEM, VMEM])(index, coupling)
    term, high, low, got = ordered(term, high, low, got)
    total = term + got

    def back(first, u, split_inverse):
        out, = call("back", functools.partial(back_kernel, first, steps // 2), [shape(m + n, half // 2)],
                    [VMEM] * 5)(u, high, low, *split_inverse)
        return out

    def quad_sum(total, far, near, last, work):
        one = swap_leaf(total, far, near)
        two = swap_leaf(total, last, near)
        done = work()
        total, done, one, two = ordered(total, done, one, two)
        total, = call("mix", mix_kernel, [shape(n, m)], [VMEM] * 3)(total, one, two)
        return total, done

    total, u = ordered(total, u)
    got = swap_leaf(total, 1)
    away0 = back(0, u, away)
    total, away0, got = ordered(total, away0, got)
    total = total + got
    got0 = swap_core(away0)

    total, u, sep_inverse, sep_parent = ordered(total, u, sep_inverse, sep_parent)
    def work():
        away1 = back(steps // 2, u, away)
        return (away1,) + tuple(call(
            "tree", tree_kernel,
            [shape(2, k, m, dtype=BF16)] * 2 + [shape(4, k, k), shape(k, m), shape(n, m + k)],
            [VMEM] * 3)(sep_inverse, sep_parent, sep_rhs))
    total, (away1, wayh, wayl, own, root, chosen) = quad_sum(total, 6, 2, 5, work)
    total = total + swap_core(total)

    total, u, away1 = ordered(total, u, away1)
    got1 = swap_core(away1)
    total, home0 = quad_sum(total, 16, 8, 24, lambda: back(0, u, home))
    total = total + swap_core(total)

    total, u = ordered(total, u)
    got = swap_leaf(total, 32)
    home1 = back(steps // 2, u, home)
    total, home1, got = ordered(total, home1, got)
    source, = call("source", source_kernel, [shape(n, m + k)], [VMEM] * 3)(total, got, chosen)
    source, home0, home1, got0, got1, root = ordered(source, home0, home1, got0, got1, root)
    other = swap_leaf(source, 96)
    base, lower, qh, ql = call("join", join_kernel,
                               [shape(n, half), shape(2 * k, half)] + [shape(k, half + m, dtype=BF16)] * 2,
                               [VMEM] * 5)(home0, home1, got0, got1, root)
    pre, solved, top = call("lower", lower_kernel, [shape(n, half), shape(2, n, k), shape(n, k)], [VMEM] * 7)(
        source, chosen, wayh, wayl, own, base, lower)
    pre, other = ordered(pre, other)
    out, sep = call("last", last_kernel, [shape(n, half), shape(levels, n, k)], [VMEM] * 8)(
        other, wayh, wayl, top, pre, solved, qh, ql)
    return (out[None], sep[None])


def solution(mesh):
    placed = (
        P("leaf", None, "sep"),
        P("leaf", "sep", None),
        P("leaf", None, None),
        P("leaf", None, None, None),
        P(),
        P(),
        P(),
    )
    return jax.shard_map(
        local,
        mesh=mesh,
        in_specs=placed,
        out_specs=(P("leaf", None, "sep"), P("leaf", None, None, None)),
        check_vma=False,
    )
```

```python
import functools

import jax
import jax.numpy as jnp
from jax import lax
from jax.experimental import pallas as pl
from jax.experimental.pallas import tpu as pltpu
from jax.sharding import PartitionSpec as P

F32, BF16 = jnp.float32, jnp.bfloat16
MIB = 1 << 20
VMEM = pl.BlockSpec(memory_space=pltpu.VMEM)
HBM = pl.BlockSpec(memory_space=pltpu.HBM)
NN = (((1,), (0,)), ((), ()))
NT = (((1,), (1,)), ((), ()))
TN = (((0,), (0,)), ((), ()))


def shape(*dims, dtype=F32):
    return jax.ShapeDtypeStruct(dims, dtype)


def dot(a, b, dims=NN):
    return lax.dot_general(a, b, dims, preferred_element_type=F32)


def split(x):
    high = x.astype(BF16)
    return high, (x - high.astype(F32)).astype(BF16)


def product(a, split_b, dims=NN):
    ah, al = split(a)
    bh, bl = split_b
    rows = a.shape[0]
    both = dot(jnp.concatenate([ah, al], axis=0), bh, dims)
    return both[:rows] + both[rows:] + dot(ah, bl, dims)


def call(name, body, outs, ins, scratch=(), limit=24):
    return pl.pallas_call(
        body,
        out_shape=outs,
        in_specs=ins,
        out_specs=[VMEM] * len(outs),
        scratch_shapes=list(scratch),
        compiler_params=pltpu.CompilerParams(vmem_limit_bytes=limit * MIB),
        name=name,
    )


def load_columns(inverse_ref, firsts, chunk, a_ref, sems):
    copies = []
    for s, first in enumerate(firsts):
        start = pl.multiple_of(first, chunk)
        copy = pltpu.make_async_copy(inverse_ref.at[:, pl.ds(start, chunk)], a_ref.at[s], sems.at[s])
        copy.start()
        copies.append(copy)
    return copies


def load_kernel(chunk, inverse_ref, ah_ref, al_ref, a_ref, sems):
    steps, half = ah_ref.shape[:2]
    firsts = [lax.axis_index("sep") * half + s * chunk for s in range(steps)]
    for s, copy in enumerate(load_columns(inverse_ref, firsts, chunk, a_ref, sems)):
        copy.wait()
        ah_ref[s], al_ref[s] = split(a_ref[s])


def paired(x):
    return jnp.concatenate(split(x), axis=0)


def one_hot(index_ref, level, rows, first):
    row = lax.broadcasted_iota(jnp.int32, (rows, index_ref.shape[2]), 0) + first
    return jnp.where(row == index_ref[level], 1.0, 0.0).astype(BF16)


def leaf_kernel(chunk, mine_ref, theirs_ref, index_ref, coupling_ref, hh_ref, hl_ref, inverse_ref, term_ref, u_ref, ah_ref, al_ref, a_ref, sems):
    n, half = mine_ref.shape
    levels, _, k = index_ref.shape
    side = lax.axis_index("sep")
    firsts = [(1 - side) * half + s * chunk for s in range(half // chunk)]
    copies = load_columns(inverse_ref, firsts, chunk, a_ref, sems)
    total = jnp.zeros((2 * n, half), F32)
    for s in range(half // chunk):
        x = paired(mine_ref[:, s * chunk:(s + 1) * chunk])
        total = total + (dot(x, hh_ref[s], NT) + dot(x, hl_ref[s], NT))
    hot = [one_hot(index_ref, level, half, side * half) for level in range(levels)]
    for s, copy in enumerate(copies):
        x = paired(theirs_ref[:, s * chunk:(s + 1) * chunk])
        copy.wait()
        ah, al = split(a_ref[s])
        ah_ref[s] = ah
        al_ref[s] = al
        total = total + (dot(x, ah, NT) + dot(x, al, NT))
    u = total[:n] + total[n:]
    u_ref[...] = u
    uh, um = split(u)
    ul = (u - uh.astype(F32) - um.astype(F32)).astype(BF16)
    parts = jnp.concatenate([uh, um, ul], axis=0)
    picked = dot(parts, jnp.concatenate(hot, axis=1))
    picked = picked[:n] + picked[n:2 * n] + picked[2 * n:]
    for level in range(levels):
        cols = slice(level * k, (level + 1) * k)
        term_ref[:, cols] = product(picked[:, cols], split(coupling_ref[level]), NT)


def spread_kernel(index_ref, coupling_ref, high_ref, low_ref):
    levels, _, k = index_ref.shape
    half = high_ref.shape[1]
    for level in range(levels):
        hot = one_hot(index_ref, level, half, lax.axis_index("sep") * half)
        ch, cl = split(coupling_ref[level])
        moved = dot(jnp.concatenate([ch, cl], axis=0), hot, NT).astype(BF16)
        high_ref[level * k:(level + 1) * k, :] = moved[:k]
        low_ref[level * k:(level + 1) * k, :] = moved[k:]


def back_kernel(first, last, u_ref, high_ref, low_ref, ah_ref, al_ref, out_ref):
    n = u_ref.shape[0]
    uh, ul = split(u_ref[...])
    low = low_ref[...]
    left = jnp.concatenate([high_ref[...], uh, ul], axis=0)
    m = low.shape[0]
    chunk = ah_ref.shape[2]
    for s in range(first, last, 2):
        taken = range(s, min(s + 2, last))
        cols = slice((s - first) * chunk, (taken[-1] + 1 - first) * chunk)
        ah = jnp.concatenate([ah_ref[i] for i in taken], axis=1)
        al = jnp.concatenate([al_ref[i] for i in taken], axis=1)
        one = dot(left, ah)
        three = dot(left[:m + n], al)
        out_ref[:m, cols] = one[:m] + dot(low, ah) + three[:m]
        out_ref[m:, cols] = one[m:m + n] + one[m + n:] + three[m:]


def square(x):
    high, low = split(x)
    return dot(high, high, TN) + dot(low, high, TN) + dot(high, low, TN)


def pair_matrices(inverse_ref, parent_ref, near, sibling, middle):
    g0 = product(parent_ref[near], split(inverse_ref[near]))
    gs = product(parent_ref[sibling], split(inverse_ref[sibling]))
    g1 = product(parent_ref[middle], split(inverse_ref[middle]))
    return g0, gs, g1, jnp.concatenate([g1, -product(g1, split(g0)), -product(g1, split(gs))], axis=1)


def tree_kernel(inverse_ref, parent_ref, rhs_ref, wayh_ref, wayl_ref, own_ref, chosen_ref):
    k = inverse_ref.shape[1]
    plane = lax.axis_index("leaf") >> 5
    near, sibling, middle = plane, plane ^ 1, 4 + (plane >> 1)
    g0, gs, g1, way = pair_matrices(inverse_ref, parent_ref, near, sibling, middle)
    wayh_ref[...], wayl_ref[...] = split(way)
    own_ref[0] = g0
    own_ref[1] = gs
    own_ref[2] = square(inverse_ref[near])
    own_ref[3] = square(inverse_ref[middle])
    own_ref[4] = g1
    chosen_ref[:, :k] = rhs_ref[middle]
    chosen_ref[:, k:2 * k] = rhs_ref[near]
    chosen_ref[:, 2 * k:3 * k] = rhs_ref[sibling]
    chosen_ref[:, 3 * k:] = rhs_ref[inverse_ref.shape[0] - 1]


def root_kernel(inverse_ref, parent_ref, own_ref, wayh_ref, wayl_ref, root_ref):
    k = inverse_ref.shape[1]
    plane = 3 - (lax.axis_index("leaf") >> 5)
    way = pair_matrices(inverse_ref, parent_ref, plane, plane ^ 1, 4 + (plane >> 1))[3]
    wayh_ref[...], wayl_ref[...] = split(way)
    h2 = square(inverse_ref[inverse_ref.shape[0] - 1])
    k1 = product(h2, split(own_ref[4]))
    root_ref[:, :k] = product(k1, split(own_ref[0]))
    root_ref[:, k:2 * k] = -k1
    root_ref[:, 2 * k:] = h2


def columns_of(refs, chunk):
    return [ref.at[:, s:s + chunk] for ref in refs for s in range(0, ref.shape[1], chunk)]


def join_kernel(chunk, mine_ref, got_ref, root_ref, base_ref, low_ref, qh_ref, ql_ref):
    k = root_ref.shape[0]
    root = root_ref[...]
    m = root.shape[1]
    width = base_ref.shape[1]
    pairs = zip(columns_of((mine_ref,), chunk), columns_of((got_ref,), chunk))
    for s, (mine_ref, got_ref) in enumerate(pairs):
        cols = slice(s * chunk, (s + 1) * chunk)
        b = mine_ref[:m, :] + got_ref[:m, :]
        base_ref[:, cols] = mine_ref[m:, :] + got_ref[m:, :]
        low_ref[:, cols] = b[:2 * k]
        qh_ref[:, cols], ql_ref[:, cols] = split(product(root, split(b)))
    qh_ref[:, width:], ql_ref[:, width:] = split(root)


def octet_kernel(total_ref, four_ref, one_ref, two_ref, three_ref, out_ref):
    own = total_ref[...] + four_ref[...]
    first = lax.axis_index("sep") == 0
    out_ref[...] = one_ref[...] + two_ref[...] + three_ref[...] + jnp.where(first, own, 0.0)


def pair_kernel(total_ref, near_ref, five_ref, six_ref, two_ref, out_ref):
    m = total_ref.shape[1]
    first = lax.axis_index("sep") == 0
    heard = five_ref[...] + six_ref[...] + two_ref[...]
    out_ref[:, :m] = jnp.where(first, total_ref[...] + heard, 0.0)
    out_ref[:, m:] = jnp.where(first, near_ref[...], heard)


def source_kernel(part_ref, got_ref, chosen_ref, out_ref):
    k = part_ref.shape[1] // 6
    own = part_ref[:, :3 * k] + got_ref[:, :3 * k]
    other = part_ref[:, 3 * k:] + got_ref[:, 3 * k:]
    out_ref[:, :k] = chosen_ref[:, :k] - own[:, k:2 * k] - other[:, k:2 * k]
    out_ref[:, k:2 * k] = chosen_ref[:, k:2 * k] - own[:, :k]
    out_ref[:, 2 * k:3 * k] = chosen_ref[:, 2 * k:3 * k] - other[:, :k]
    out_ref[:, 3 * k:] = own[:, 2 * k:] + other[:, 2 * k:]


def lower_kernel(source_ref, chosen_ref, wayh_ref, wayl_ref, own_ref, base_ref, low_ref, pre_ref, solved_ref, top_ref):
    k = own_ref.shape[1]
    t1, s0, sb = source_ref[:, :k], source_ref[:, k:2 * k], source_ref[:, 2 * k:3 * k]
    c0 = product(s0, split(own_ref[2]))
    s1 = t1 - product(s0, split(own_ref[0]), NT) - product(sb, split(own_ref[1]), NT)
    c1 = product(s1, split(own_ref[3]))
    c0 = c0 - product(c1, split(own_ref[0]))
    solved_ref[0] = c0
    solved_ref[1] = c1
    pre_ref[...] = base_ref[...] - product(jnp.concatenate([c0, c1], axis=1), split(low_ref[...]))
    up = product(source_ref[:, :3 * k], (wayh_ref[...], wayl_ref[...]), NT)
    top_ref[...] = chosen_ref[:, 3 * k:] - source_ref[:, 3 * k:] - up


def last_kernel(other_ref, wayh_ref, wayl_ref, top_ref, pre_ref, solved_ref, qh_ref, ql_ref, out_ref, sep_ref):
    k = top_ref.shape[1]
    width = pre_ref.shape[1]
    up = product(other_ref[:, :3 * k], (wayh_ref[...], wayl_ref[...]), NT)
    s2 = top_ref[...] - other_ref[:, 3 * k:] - up
    add = product(s2, (qh_ref[...], ql_ref[...]))
    out_ref[...] = pre_ref[...] - add[:, :width]
    sep_ref[0] = solved_ref[0] + add[:, width:width + k]
    sep_ref[1] = solved_ref[1] + add[:, width + k:width + 2 * k]
    sep_ref[2] = add[:, width + 2 * k:]


def swap_core(x):
    return lax.ppermute(x, "sep", [(0, 1), (1, 0)])


def swap_leaf(x, mask, first_mask=None):
    masks = (mask if first_mask is None else first_mask, mask)
    count = 2 * lax.axis_size("leaf")
    return lax.ppermute(x, ("leaf", "sep"), [(i, i ^ 2 * masks[i % 2]) for i in range(count)])


def ordered(*arrays):
    return lax.optimization_barrier(arrays)


def local(leaf_rhs, leaf_inverse, skeleton_index, leaf_coupling, sep_rhs, sep_inverse, sep_parent):
    mine, coupling = leaf_rhs[0], leaf_coupling[0]
    index = jnp.transpose(skeleton_index, (1, 0, 2))
    inverse = leaf_inverse[0]
    n, half = mine.shape
    levels, _, k = index.shape
    m = levels * k
    chunk = 256
    steps = half // chunk
    slots = [pltpu.VMEM((steps, half, chunk), F32), pltpu.SemaphoreType.DMA((steps,))]
    parts = [shape(steps, half, chunk, dtype=BF16)] * 2
    theirs = swap_core(mine)
    home = call("load", functools.partial(load_kernel, chunk), parts, [HBM], slots, limit=48)(inverse)
    term, u, *away = call("leaf", functools.partial(leaf_kernel, chunk), [shape(n, m), shape(n, half)] + parts,
                          [VMEM] * 6 + [HBM], slots, limit=43)(mine, theirs, index, coupling, *home, inverse)
    term, index, coupling = ordered(term, index, coupling)
    got = swap_core(term)
    high, low = call("spread", spread_kernel, [shape(m, half, dtype=BF16)] * 2, [VMEM, VMEM])(index, coupling)
    term, high, low, got = ordered(term, high, low, got)
    total = term + got

    def back(u, split_inverse, first, last):
        out, = call("back", functools.partial(back_kernel, first, last), [shape(m + n, (last - first) * chunk)],
                    [VMEM] * 5)(u, high, low, *split_inverse)
        return out

    total, u = ordered(total, u)
    heard = [swap_leaf(total, *masks) for masks in ((1, 1), (24, 8), (16, 25), (17, 9))]
    sent0 = back(u, away, 0, steps)
    total, sent0, *heard = ordered(total, sent0, *heard)
    total, = call("octet", octet_kernel, [shape(n, m)], [VMEM] * 5)(total, *heard)
    total, sep_inverse, sep_parent, sep_rhs = ordered(total, sep_inverse, sep_parent, sep_rhs)
    got = swap_core(total)
    wayh, wayl, own, chosen = call(
        "tree", tree_kernel, [shape(k, m, dtype=BF16)] * 2 + [shape(5, k, k), shape(n, m + k)],
        [VMEM] * 3)(sep_inverse, sep_parent, sep_rhs)
    total, got, own = ordered(total, got, own)
    total = total + got

    total, u, sent0 = ordered(total, u, sent0)
    received0 = swap_core(sent0)
    heard = [swap_leaf(total, *masks) for masks in ((1, 32), (34, 2), (38, 6), (37, 5))]
    kept0 = back(u, home, 0, steps)
    total, kept0, *heard = ordered(total, kept0, *heard)
    part, = call("pair", pair_kernel, [shape(n, 2 * m)], [VMEM] * 5)(total, *heard)
    part, own, sep_inverse, sep_parent = ordered(part, own, sep_inverse, sep_parent)
    got = swap_core(part)
    otherh, otherl, root = call(
        "root", root_kernel, [shape(k, m, dtype=BF16)] * 2 + [shape(k, m)], [VMEM] * 3)(sep_inverse, sep_parent, own)
    part, got, root = ordered(part, got, root)
    source, = call("source", source_kernel, [shape(n, m + k)], [VMEM] * 3)(part, got, chosen)

    source, u, root = ordered(source, u, root)
    other = swap_leaf(source, 96)
    base, lower, qh, ql = call("join", functools.partial(join_kernel, chunk),
                               [shape(n, half), shape(2 * k, half)] + [shape(k, half + m, dtype=BF16)] * 2,
                               [VMEM] * 3)(kept0, received0, root)
    pre, solved, top = call("lower", lower_kernel, [shape(n, half), shape(2, n, k), shape(n, k)], [VMEM] * 7)(
        source, chosen, wayh, wayl, own, base, lower)
    pre, other = ordered(pre, other)
    out, sep = call("last", last_kernel, [shape(n, half), shape(levels, n, k)], [VMEM] * 8)(
        other, otherh, otherl, top, pre, solved, qh, ql)
    return (out[None], sep[None])


def solution(mesh):
    placed = (
        P("leaf", None, "sep"),
        P("leaf", "sep", None),
        P("leaf", None, None),
        P("leaf", None, None, None),
        P(),
        P(),
        P(),
    )
    return jax.shard_map(
        local,
        mesh=mesh,
        in_specs=placed,
        out_specs=(P("leaf", None, "sep"), P("leaf", None, None, None)),
        check_vma=False,
    )
```

```python
import functools

import jax
import jax.numpy as jnp
from jax import lax
from jax.experimental import pallas as pl
from jax.experimental.pallas import tpu as pltpu
from jax.sharding import PartitionSpec as P

F32, BF16 = jnp.float32, jnp.bfloat16
MIB = 1 << 20
VMEM = pl.BlockSpec(memory_space=pltpu.VMEM)
HBM = pl.BlockSpec(memory_space=pltpu.HBM)
NN = (((1,), (0,)), ((), ()))
NT = (((1,), (1,)), ((), ()))
TN = (((0,), (0,)), ((), ()))


def shape(*dims, dtype=F32):
    return jax.ShapeDtypeStruct(dims, dtype)


def dot(a, b, dims=NN):
    return lax.dot_general(a, b, dims, preferred_element_type=F32)


def split(x):
    high = x.astype(BF16)
    return high, (x - high.astype(F32)).astype(BF16)


def product(a, split_b, dims=NN):
    ah, al = split(a)
    bh, bl = split_b
    rows = a.shape[0]
    both = dot(jnp.concatenate([ah, al], axis=0), bh, dims)
    return both[:rows] + both[rows:] + dot(ah, bl, dims)


def call(name, body, outs, ins, scratch=(), limit=24):
    return pl.pallas_call(
        body,
        out_shape=outs,
        in_specs=ins,
        out_specs=[VMEM] * len(outs),
        scratch_shapes=list(scratch),
        compiler_params=pltpu.CompilerParams(vmem_limit_bytes=limit * MIB),
        name=name,
    )


def load_columns(inverse_ref, firsts, chunk, a_ref, sems):
    copies = []
    for s, first in enumerate(firsts):
        start = pl.multiple_of(first, chunk)
        copy = pltpu.make_async_copy(inverse_ref.at[:, pl.ds(start, chunk)], a_ref.at[s], sems.at[s])
        copy.start()
        copies.append(copy)
    return copies


def load_kernel(chunk, inverse_ref, ah_ref, al_ref, a_ref, sems):
    steps, half = ah_ref.shape[:2]
    firsts = [lax.axis_index("sep") * half + s * chunk for s in range(steps)]
    for s, copy in enumerate(load_columns(inverse_ref, firsts, chunk, a_ref, sems)):
        copy.wait()
        ah_ref[s], al_ref[s] = split(a_ref[s])


def paired(x):
    return jnp.concatenate(split(x), axis=0)


def one_hot(index_ref, level, rows, first):
    row = lax.broadcasted_iota(jnp.int32, (rows, index_ref.shape[2]), 0) + first
    return jnp.where(row == index_ref[level], 1.0, 0.0).astype(BF16)


def leaf_kernel(chunk, mine_ref, theirs_ref, index_ref, coupling_ref, eh_ref, el_ref, inverse_ref, term_ref, u_ref, rh_ref, rl_ref, ah_ref, al_ref, a_ref, sems):
    n, half = mine_ref.shape
    levels, _, k = index_ref.shape
    side = lax.axis_index("sep")
    early, rest = eh_ref.shape[0], rh_ref.shape[0]
    firsts = [side * half + (early + s) * chunk for s in range(rest)]
    firsts += [(1 - side) * half + s * chunk for s in range(half // chunk)]
    copies = load_columns(inverse_ref, firsts, chunk, a_ref, sems)
    total = jnp.zeros((2 * n, half), F32)
    for s in range(early):
        x = paired(mine_ref[:, s * chunk:(s + 1) * chunk])
        total = total + (dot(x, eh_ref[s], NT) + dot(x, el_ref[s], NT))
    hot = [one_hot(index_ref, level, half, side * half) for level in range(levels)]
    for s, copy in enumerate(copies):
        mine = s < rest
        x_ref, high_ref, low_ref = (mine_ref, rh_ref, rl_ref) if mine else (theirs_ref, ah_ref, al_ref)
        to = s if mine else s - rest
        at = early + s if mine else to
        x = paired(x_ref[:, at * chunk:(at + 1) * chunk])
        copy.wait()
        ah, al = split(a_ref[s])
        high_ref[to] = ah
        low_ref[to] = al
        total = total + (dot(x, ah, NT) + dot(x, al, NT))
    u = total[:n] + total[n:]
    u_ref[...] = u
    uh, um = split(u)
    ul = (u - uh.astype(F32) - um.astype(F32)).astype(BF16)
    parts = jnp.concatenate([uh, um, ul], axis=0)
    picked = dot(parts, jnp.concatenate(hot, axis=1))
    picked = picked[:n] + picked[n:2 * n] + picked[2 * n:]
    for level in range(levels):
        cols = slice(level * k, (level + 1) * k)
        term_ref[:, cols] = product(picked[:, cols], split(coupling_ref[level]), NT)


def spread_kernel(index_ref, coupling_ref, high_ref, low_ref):
    levels, _, k = index_ref.shape
    half = high_ref.shape[1]
    for level in range(levels):
        hot = one_hot(index_ref, level, half, lax.axis_index("sep") * half)
        ch, cl = split(coupling_ref[level])
        moved = dot(jnp.concatenate([ch, cl], axis=0), hot, NT).astype(BF16)
        high_ref[level * k:(level + 1) * k, :] = moved[:k]
        low_ref[level * k:(level + 1) * k, :] = moved[k:]


def back_kernel(u_ref, high_ref, low_ref, *refs):
    *refs, out_ref = refs
    n = u_ref.shape[0]
    uh, ul = split(u_ref[...])
    low = low_ref[...]
    left = jnp.concatenate([high_ref[...], uh, ul], axis=0)
    m = low.shape[0]
    chunk = refs[0].shape[2]
    highs, lows = [
        [ref.at[s] for ref in some for s in range(ref.shape[0])] for some in (refs[::2], refs[1::2])
    ]
    for s in range(0, len(highs), 2):
        cols = slice(s * chunk, (s + 2) * chunk)
        ah = jnp.concatenate([ref[...] for ref in highs[s:s + 2]], axis=1)
        al = jnp.concatenate([ref[...] for ref in lows[s:s + 2]], axis=1)
        one = dot(left, ah)
        three = dot(left[:m + n], al)
        out_ref[:m, cols] = one[:m] + dot(low, ah) + three[:m]
        out_ref[m:, cols] = one[m:m + n] + one[m + n:] + three[m:]


def square(x):
    high, low = split(x)
    return dot(high, high, TN) + dot(low, high, TN) + dot(high, low, TN)


def pair_matrices(inverse_ref, parent_ref, near, sibling, middle):
    g0 = product(parent_ref[near], split(inverse_ref[near]))
    gs = product(parent_ref[sibling], split(inverse_ref[sibling]))
    g1 = product(parent_ref[middle], split(inverse_ref[middle]))
    return g0, gs, g1, jnp.concatenate([g1, -product(g1, split(g0)), -product(g1, split(gs))], axis=1)


def tree_kernel(inverse_ref, parent_ref, rhs_ref, wayh_ref, wayl_ref, own_ref, chosen_ref):
    k = inverse_ref.shape[1]
    plane = lax.axis_index("leaf") >> 5
    near, sibling, middle = plane, plane ^ 1, 4 + (plane >> 1)
    g0, gs, g1, way = pair_matrices(inverse_ref, parent_ref, near, sibling, middle)
    wayh_ref[...], wayl_ref[...] = split(way)
    own_ref[0] = g0
    own_ref[1] = gs
    own_ref[2] = square(inverse_ref[near])
    own_ref[3] = square(inverse_ref[middle])
    own_ref[4] = g1
    chosen_ref[:, :k] = rhs_ref[middle]
    chosen_ref[:, k:2 * k] = rhs_ref[near]
    chosen_ref[:, 2 * k:3 * k] = rhs_ref[sibling]
    chosen_ref[:, 3 * k:] = rhs_ref[inverse_ref.shape[0] - 1]


def root_kernel(inverse_ref, parent_ref, own_ref, wayh_ref, wayl_ref, root_ref):
    k = inverse_ref.shape[1]
    plane = 3 - (lax.axis_index("leaf") >> 5)
    way = pair_matrices(inverse_ref, parent_ref, plane, plane ^ 1, 4 + (plane >> 1))[3]
    wayh_ref[...], wayl_ref[...] = split(way)
    h2 = square(inverse_ref[inverse_ref.shape[0] - 1])
    k1 = product(h2, split(own_ref[4]))
    root_ref[:, :k] = product(k1, split(own_ref[0]))
    root_ref[:, k:2 * k] = -k1
    root_ref[:, 2 * k:] = h2


def columns_of(refs, chunk):
    return [ref.at[:, s:s + chunk] for ref in refs for s in range(0, ref.shape[1], chunk)]


def join_kernel(chunk, mine_ref, got_ref, root_ref, base_ref, low_ref, qh_ref, ql_ref):
    k = root_ref.shape[0]
    root = root_ref[...]
    m = root.shape[1]
    width = base_ref.shape[1]
    pairs = zip(columns_of((mine_ref,), chunk), columns_of((got_ref,), chunk))
    for s, (mine_ref, got_ref) in enumerate(pairs):
        cols = slice(s * chunk, (s + 1) * chunk)
        b = mine_ref[:m, :] + got_ref[:m, :]
        base_ref[:, cols] = mine_ref[m:, :] + got_ref[m:, :]
        low_ref[:, cols] = b[:2 * k]
        qh_ref[:, cols], ql_ref[:, cols] = split(product(root, split(b)))
    qh_ref[:, width:], ql_ref[:, width:] = split(root)


def octet_kernel(total_ref, four_ref, one_ref, two_ref, three_ref, out_ref):
    own = total_ref[...] + four_ref[...]
    first = lax.axis_index("sep") == 0
    out_ref[...] = one_ref[...] + two_ref[...] + three_ref[...] + jnp.where(first, own, 0.0)


def pair_kernel(total_ref, near_ref, five_ref, six_ref, two_ref, out_ref):
    m = total_ref.shape[1]
    first = lax.axis_index("sep") == 0
    heard = five_ref[...] + six_ref[...] + two_ref[...]
    out_ref[:, :m] = jnp.where(first, total_ref[...] + heard, 0.0)
    out_ref[:, m:] = jnp.where(first, near_ref[...], heard)


def source_kernel(part_ref, got_ref, chosen_ref, out_ref):
    k = part_ref.shape[1] // 6
    own = part_ref[:, :3 * k] + got_ref[:, :3 * k]
    other = part_ref[:, 3 * k:] + got_ref[:, 3 * k:]
    out_ref[:, :k] = chosen_ref[:, :k] - own[:, k:2 * k] - other[:, k:2 * k]
    out_ref[:, k:2 * k] = chosen_ref[:, k:2 * k] - own[:, :k]
    out_ref[:, 2 * k:3 * k] = chosen_ref[:, 2 * k:3 * k] - other[:, :k]
    out_ref[:, 3 * k:] = own[:, 2 * k:] + other[:, 2 * k:]


def lower_kernel(source_ref, chosen_ref, wayh_ref, wayl_ref, own_ref, base_ref, low_ref, pre_ref, solved_ref, top_ref):
    k = own_ref.shape[1]
    t1, s0, sb = source_ref[:, :k], source_ref[:, k:2 * k], source_ref[:, 2 * k:3 * k]
    c0 = product(s0, split(own_ref[2]))
    s1 = t1 - product(s0, split(own_ref[0]), NT) - product(sb, split(own_ref[1]), NT)
    c1 = product(s1, split(own_ref[3]))
    c0 = c0 - product(c1, split(own_ref[0]))
    solved_ref[0] = c0
    solved_ref[1] = c1
    pre_ref[...] = base_ref[...] - product(jnp.concatenate([c0, c1], axis=1), split(low_ref[...]))
    up = product(source_ref[:, :3 * k], (wayh_ref[...], wayl_ref[...]), NT)
    top_ref[...] = chosen_ref[:, 3 * k:] - source_ref[:, 3 * k:] - up


def last_kernel(other_ref, wayh_ref, wayl_ref, top_ref, pre_ref, solved_ref, qh_ref, ql_ref, out_ref, sep_ref):
    k = top_ref.shape[1]
    width = pre_ref.shape[1]
    up = product(other_ref[:, :3 * k], (wayh_ref[...], wayl_ref[...]), NT)
    s2 = top_ref[...] - other_ref[:, 3 * k:] - up
    add = product(s2, (qh_ref[...], ql_ref[...]))
    out_ref[...] = pre_ref[...] - add[:, :width]
    sep_ref[0] = solved_ref[0] + add[:, width:width + k]
    sep_ref[1] = solved_ref[1] + add[:, width + k:width + 2 * k]
    sep_ref[2] = add[:, width + 2 * k:]


def swap_core(x):
    return lax.ppermute(x, "sep", [(0, 1), (1, 0)])


def swap_leaf(x, mask, first_mask=None):
    masks = (mask if first_mask is None else first_mask, mask)
    count = 2 * lax.axis_size("leaf")
    return lax.ppermute(x, ("leaf", "sep"), [(i, i ^ 2 * masks[i % 2]) for i in range(count)])


def ordered(*arrays):
    return lax.optimization_barrier(arrays)


def local(leaf_rhs, leaf_inverse, skeleton_index, leaf_coupling, sep_rhs, sep_inverse, sep_parent):
    mine, coupling = leaf_rhs[0], leaf_coupling[0]
    index = jnp.transpose(skeleton_index, (1, 0, 2))
    inverse = leaf_inverse[0]
    n, half = mine.shape
    levels, _, k = index.shape
    m = levels * k
    chunk = 256
    steps = half // chunk
    early = 1
    slots = lambda count: [pltpu.VMEM((count, half, chunk), F32), pltpu.SemaphoreType.DMA((count,))]
    parts = lambda count: [shape(count, half, chunk, dtype=BF16)] * 2
    theirs = swap_core(mine)
    first = call("load", functools.partial(load_kernel, chunk), parts(early), [HBM], slots(early), limit=51)(inverse)
    term, u, *rest = call(
        "leaf", functools.partial(leaf_kernel, chunk),
        [shape(n, m), shape(n, half)] + parts(steps - early) + parts(steps),
        [VMEM] * 6 + [HBM], slots(2 * steps - early), limit=44)(mine, theirs, index, coupling, *first, inverse)
    home, away = (*first, *rest[:2]), rest[2:]
    term, index, coupling = ordered(term, index, coupling)
    got = swap_core(term)
    high, low = call("spread", spread_kernel, [shape(m, half, dtype=BF16)] * 2, [VMEM, VMEM])(index, coupling)
    term, high, low, got = ordered(term, high, low, got)
    total = term + got

    def back(u, split_inverse):
        out, = call("back", back_kernel, [shape(m + n, half)], [VMEM] * (3 + len(split_inverse)))(
            u, high, low, *split_inverse)
        return out

    total, u = ordered(total, u)
    heard = [swap_leaf(total, *masks) for masks in ((1, 1), (24, 8), (16, 25), (17, 9))]
    sent0 = back(u, away)
    total, sent0, *heard = ordered(total, sent0, *heard)
    total, = call("octet", octet_kernel, [shape(n, m)], [VMEM] * 5)(total, *heard)
    total, sep_inverse, sep_parent, sep_rhs = ordered(total, sep_inverse, sep_parent, sep_rhs)
    got = swap_core(total)
    wayh, wayl, own, chosen = call(
        "tree", tree_kernel, [shape(k, m, dtype=BF16)] * 2 + [shape(5, k, k), shape(n, m + k)],
        [VMEM] * 3)(sep_inverse, sep_parent, sep_rhs)
    total, got, own = ordered(total, got, own)
    total = total + got

    total, u, sent0 = ordered(total, u, sent0)
    received0 = swap_core(sent0)
    heard = [swap_leaf(total, *masks) for masks in ((1, 32), (34, 2), (38, 6), (37, 5))]
    kept0 = back(u, home)
    total, kept0, *heard = ordered(total, kept0, *heard)
    part, = call("pair", pair_kernel, [shape(n, 2 * m)], [VMEM] * 5)(total, *heard)
    part, own, sep_inverse, sep_parent = ordered(part, own, sep_inverse, sep_parent)
    got = swap_core(part)
    otherh, otherl, root = call(
        "root", root_kernel, [shape(k, m, dtype=BF16)] * 2 + [shape(k, m)], [VMEM] * 3)(sep_inverse, sep_parent, own)
    part, got, root = ordered(part, got, root)
    source, = call("source", source_kernel, [shape(n, m + k)], [VMEM] * 3)(part, got, chosen)

    source, u, root = ordered(source, u, root)
    other = swap_leaf(source, 96)
    base, lower, qh, ql = call("join", functools.partial(join_kernel, chunk),
                               [shape(n, half), shape(2 * k, half)] + [shape(k, half + m, dtype=BF16)] * 2,
                               [VMEM] * 3)(kept0, received0, root)
    pre, solved, top = call("lower", lower_kernel, [shape(n, half), shape(2, n, k), shape(n, k)], [VMEM] * 7)(
        source, chosen, wayh, wayl, own, base, lower)
    pre, other = ordered(pre, other)
    out, sep = call("last", last_kernel, [shape(n, half), shape(levels, n, k)], [VMEM] * 8)(
        other, otherh, otherl, top, pre, solved, qh, ql)
    return (out[None], sep[None])


def solution(mesh):
    placed = (
        P("leaf", None, "sep"),
        P("leaf", "sep", None),
        P("leaf", None, None),
        P("leaf", None, None, None),
        P(),
        P(),
        P(),
    )
    return jax.shard_map(
        local,
        mesh=mesh,
        in_specs=placed,
        out_specs=(P("leaf", None, "sep"), P("leaf", None, None, None)),
        check_vma=False,
    )
```

```python
import functools

import jax
import jax.numpy as jnp
from jax import lax
from jax.experimental import pallas as pl
from jax.experimental.pallas import tpu as pltpu
from jax.sharding import PartitionSpec as P

F32, BF16 = jnp.float32, jnp.bfloat16
MIB = 1 << 20
VMEM = pl.BlockSpec(memory_space=pltpu.VMEM)
HBM = pl.BlockSpec(memory_space=pltpu.HBM)
NN = (((1,), (0,)), ((), ()))
NT = (((1,), (1,)), ((), ()))
TN = (((0,), (0,)), ((), ()))


def shape(*dims, dtype=F32):
    return jax.ShapeDtypeStruct(dims, dtype)


def dot(a, b, dims=NN):
    return lax.dot_general(a, b, dims, preferred_element_type=F32)


def split(x):
    high = x.astype(BF16)
    return high, (x - high.astype(F32)).astype(BF16)


def product(a, split_b, dims=NN):
    ah, al = split(a)
    bh, bl = split_b
    rows = a.shape[0]
    both = dot(jnp.concatenate([ah, al], axis=0), bh, dims)
    return both[:rows] + both[rows:] + dot(ah, bl, dims)


def call(name, body, outs, ins, scratch=(), limit=24):
    return pl.pallas_call(
        body,
        out_shape=outs,
        in_specs=ins,
        out_specs=[VMEM] * len(outs),
        scratch_shapes=list(scratch),
        compiler_params=pltpu.CompilerParams(vmem_limit_bytes=limit * MIB),
        name=name,
    )


def load_columns(inverse_ref, firsts, chunk, a_ref, sems):
    copies = []
    for s, first in enumerate(firsts):
        start = pl.multiple_of(first, chunk)
        copy = pltpu.make_async_copy(inverse_ref.at[:, pl.ds(start, chunk)], a_ref.at[s], sems.at[s])
        copy.start()
        copies.append(copy)
    return copies


def load_kernel(chunk, inverse_ref, ah_ref, al_ref, a_ref, sems):
    steps, half = ah_ref.shape[:2]
    firsts = [lax.axis_index("sep") * half + s * chunk for s in range(steps)]
    for s, copy in enumerate(load_columns(inverse_ref, firsts, chunk, a_ref, sems)):
        copy.wait()
        ah_ref[s], al_ref[s] = split(a_ref[s])


def paired(x):
    return jnp.concatenate(split(x), axis=0)


def one_hot(index_ref, level, rows, first):
    row = lax.broadcasted_iota(jnp.int32, (rows, index_ref.shape[2]), 0) + first
    return jnp.where(row == index_ref[level], 1.0, 0.0).astype(BF16)


def leaf_kernel(chunk, mine_ref, theirs_ref, index_ref, coupling_ref, eh_ref, el_ref, inverse_ref, term_ref, u_ref, rh_ref, rl_ref, ah_ref, al_ref, a_ref, sems):
    n, half = mine_ref.shape
    levels, _, k = index_ref.shape
    side = lax.axis_index("sep")
    early, rest = eh_ref.shape[0], rh_ref.shape[0]
    firsts = [side * half + (early + s) * chunk for s in range(rest)]
    firsts += [(1 - side) * half + s * chunk for s in range(half // chunk)]
    copies = load_columns(inverse_ref, firsts, chunk, a_ref, sems)
    total = jnp.zeros((2 * n, half), F32)
    for s in range(early):
        x = paired(mine_ref[:, s * chunk:(s + 1) * chunk])
        total = total + (dot(x, eh_ref[s], NT) + dot(x, el_ref[s], NT))
    hot = [one_hot(index_ref, level, half, side * half) for level in range(levels)]
    for s, copy in enumerate(copies):
        mine = s < rest
        x_ref, high_ref, low_ref = (mine_ref, rh_ref, rl_ref) if mine else (theirs_ref, ah_ref, al_ref)
        to = s if mine else s - rest
        at = early + s if mine else to
        x = paired(x_ref[:, at * chunk:(at + 1) * chunk])
        copy.wait()
        ah, al = split(a_ref[s])
        high_ref[to] = ah
        low_ref[to] = al
        total = total + (dot(x, ah, NT) + dot(x, al, NT))
    u = total[:n] + total[n:]
    u_ref[...] = u
    uh, um = split(u)
    ul = (u - uh.astype(F32) - um.astype(F32)).astype(BF16)
    parts = jnp.concatenate([uh, um, ul], axis=0)
    picked = dot(parts, jnp.concatenate(hot, axis=1))
    picked = picked[:n] + picked[n:2 * n] + picked[2 * n:]
    for level in range(levels):
        cols = slice(level * k, (level + 1) * k)
        term_ref[:, cols] = product(picked[:, cols], split(coupling_ref[level]), NT)


def spread_kernel(index_ref, coupling_ref, high_ref, low_ref):
    levels, _, k = index_ref.shape
    half = high_ref.shape[1]
    for level in range(levels):
        hot = one_hot(index_ref, level, half, lax.axis_index("sep") * half)
        ch, cl = split(coupling_ref[level])
        moved = dot(jnp.concatenate([ch, cl], axis=0), hot, NT).astype(BF16)
        high_ref[level * k:(level + 1) * k, :] = moved[:k]
        low_ref[level * k:(level + 1) * k, :] = moved[k:]


def back_kernel(u_ref, high_ref, low_ref, *refs):
    *refs, out_ref = refs
    n = u_ref.shape[0]
    uh, ul = split(u_ref[...])
    low = low_ref[...]
    left = jnp.concatenate([high_ref[...], uh, ul], axis=0)
    m = low.shape[0]
    chunk = refs[0].shape[2]
    highs, lows = [
        [ref.at[s] for ref in some for s in range(ref.shape[0])] for some in (refs[::2], refs[1::2])
    ]
    for s in range(0, len(highs), 2):
        cols = slice(s * chunk, (s + 2) * chunk)
        ah = jnp.concatenate([ref[...] for ref in highs[s:s + 2]], axis=1)
        al = jnp.concatenate([ref[...] for ref in lows[s:s + 2]], axis=1)
        one = dot(left, ah)
        three = dot(left[:m + n], al)
        out_ref[:m, cols] = one[:m] + dot(low, ah) + three[:m]
        out_ref[m:, cols] = one[m:m + n] + one[m + n:] + three[m:]


def square(x):
    high, low = split(x)
    return dot(high, high, TN) + dot(low, high, TN) + dot(high, low, TN)


def pair_matrices(inverse_ref, parent_ref, near, sibling, middle):
    g0 = product(parent_ref[near], split(inverse_ref[near]))
    gs = product(parent_ref[sibling], split(inverse_ref[sibling]))
    g1 = product(parent_ref[middle], split(inverse_ref[middle]))
    return g0, gs, g1, jnp.concatenate([g1, -product(g1, split(g0)), -product(g1, split(gs))], axis=1)


def tree_kernel(inverse_ref, parent_ref, rhs_ref, wayh_ref, wayl_ref, own_ref, chosen_ref):
    k = inverse_ref.shape[1]
    plane = lax.axis_index("leaf") >> 5
    near, sibling, middle = plane, plane ^ 1, 4 + (plane >> 1)
    g0, gs, g1, way = pair_matrices(inverse_ref, parent_ref, near, sibling, middle)
    wayh_ref[...], wayl_ref[...] = split(way)
    own_ref[0] = g0
    own_ref[1] = gs
    own_ref[2] = square(inverse_ref[near])
    own_ref[3] = square(inverse_ref[middle])
    own_ref[4] = g1
    chosen_ref[:, :k] = rhs_ref[middle]
    chosen_ref[:, k:2 * k] = rhs_ref[near]
    chosen_ref[:, 2 * k:3 * k] = rhs_ref[sibling]
    chosen_ref[:, 3 * k:] = rhs_ref[inverse_ref.shape[0] - 1]


def root_kernel(inverse_ref, parent_ref, own_ref, wayh_ref, wayl_ref, root_ref):
    k = inverse_ref.shape[1]
    plane = 3 - (lax.axis_index("leaf") >> 5)
    way = pair_matrices(inverse_ref, parent_ref, plane, plane ^ 1, 4 + (plane >> 1))[3]
    wayh_ref[...], wayl_ref[...] = split(way)
    h2 = square(inverse_ref[inverse_ref.shape[0] - 1])
    k1 = product(h2, split(own_ref[4]))
    root_ref[:, :k] = product(k1, split(own_ref[0]))
    root_ref[:, k:2 * k] = -k1
    root_ref[:, 2 * k:] = h2


def columns_of(refs, chunk):
    return [ref.at[:, s:s + chunk] for ref in refs for s in range(0, ref.shape[1], chunk)]


def join_kernel(chunk, mine_ref, got_ref, root_ref, base_ref, low_ref, qh_ref, ql_ref):
    k = root_ref.shape[0]
    root = root_ref[...]
    m = root.shape[1]
    width = base_ref.shape[1]
    pairs = zip(columns_of((mine_ref,), chunk), columns_of((got_ref,), chunk))
    for s, (mine_ref, got_ref) in enumerate(pairs):
        cols = slice(s * chunk, (s + 1) * chunk)
        b = mine_ref[:m, :] + got_ref[:m, :]
        base_ref[:, cols] = mine_ref[m:, :] + got_ref[m:, :]
        low_ref[:, cols] = b[:2 * k]
        qh_ref[:, cols], ql_ref[:, cols] = split(product(root, split(b)))
    qh_ref[:, width:], ql_ref[:, width:] = split(root)


def octet_kernel(total_ref, four_ref, one_ref, two_ref, three_ref, out_ref):
    own = total_ref[...] + four_ref[...]
    first = lax.axis_index("sep") == 0
    out_ref[...] = one_ref[...] + two_ref[...] + three_ref[...] + jnp.where(first, own, 0.0)


def pair_kernel(total_ref, near_ref, two_ref, six_ref, five_ref, out_ref):
    own = jnp.where(lax.axis_index("sep") == 0, total_ref[...], near_ref[...])
    out_ref[...] = own + two_ref[...] + six_ref[...] + five_ref[...]


def source_kernel(part_ref, got_ref, chosen_ref, out_ref):
    k = part_ref.shape[1] // 3
    first = lax.axis_index("sep") == 0
    part, got = part_ref[...], got_ref[...]
    own, other = jnp.where(first, part, got), jnp.where(first, got, part)
    out_ref[:, :k] = chosen_ref[:, :k] - own[:, k:2 * k] - other[:, k:2 * k]
    out_ref[:, k:2 * k] = chosen_ref[:, k:2 * k] - own[:, :k]
    out_ref[:, 2 * k:3 * k] = chosen_ref[:, 2 * k:3 * k] - other[:, :k]
    out_ref[:, 3 * k:] = own[:, 2 * k:] + other[:, 2 * k:]


def lower_kernel(source_ref, chosen_ref, wayh_ref, wayl_ref, own_ref, base_ref, low_ref, pre_ref, solved_ref, top_ref):
    k = own_ref.shape[1]
    t1, s0, sb = source_ref[:, :k], source_ref[:, k:2 * k], source_ref[:, 2 * k:3 * k]
    c0 = product(s0, split(own_ref[2]))
    s1 = t1 - product(s0, split(own_ref[0]), NT) - product(sb, split(own_ref[1]), NT)
    c1 = product(s1, split(own_ref[3]))
    c0 = c0 - product(c1, split(own_ref[0]))
    solved_ref[0] = c0
    solved_ref[1] = c1
    pre_ref[...] = base_ref[...] - product(jnp.concatenate([c0, c1], axis=1), split(low_ref[...]))
    up = product(source_ref[:, :3 * k], (wayh_ref[...], wayl_ref[...]), NT)
    top_ref[...] = chosen_ref[:, 3 * k:] - source_ref[:, 3 * k:] - up


def last_kernel(other_ref, wayh_ref, wayl_ref, top_ref, pre_ref, solved_ref, qh_ref, ql_ref, out_ref, sep_ref):
    k = top_ref.shape[1]
    width = pre_ref.shape[1]
    up = product(other_ref[:, :3 * k], (wayh_ref[...], wayl_ref[...]), NT)
    s2 = top_ref[...] - other_ref[:, 3 * k:] - up
    add = product(s2, (qh_ref[...], ql_ref[...]))
    out_ref[...] = pre_ref[...] - add[:, :width]
    sep_ref[0] = solved_ref[0] + add[:, width:width + k]
    sep_ref[1] = solved_ref[1] + add[:, width + k:width + 2 * k]
    sep_ref[2] = add[:, width + 2 * k:]


def swap_core(x):
    return lax.ppermute(x, "sep", [(0, 1), (1, 0)])


def swap_leaf(x, mask, first_mask=None):
    masks = (mask if first_mask is None else first_mask, mask)
    count = 2 * lax.axis_size("leaf")
    return lax.ppermute(x, ("leaf", "sep"), [(i, i ^ 2 * masks[i % 2]) for i in range(count)])


def ordered(*arrays):
    return lax.optimization_barrier(arrays)


def local(leaf_rhs, leaf_inverse, skeleton_index, leaf_coupling, sep_rhs, sep_inverse, sep_parent):
    mine, coupling = leaf_rhs[0], leaf_coupling[0]
    index = jnp.transpose(skeleton_index, (1, 0, 2))
    inverse = leaf_inverse[0]
    n, half = mine.shape
    levels, _, k = index.shape
    m = levels * k
    chunk = 256
    steps = half // chunk
    early = 1
    slots = lambda count: [pltpu.VMEM((count, half, chunk), F32), pltpu.SemaphoreType.DMA((count,))]
    parts = lambda count: [shape(count, half, chunk, dtype=BF16)] * 2
    theirs = swap_core(mine)
    first = call("load", functools.partial(load_kernel, chunk), parts(early), [HBM], slots(early), limit=51)(inverse)
    term, u, *rest = call(
        "leaf", functools.partial(leaf_kernel, chunk),
        [shape(n, m), shape(n, half)] + parts(steps - early) + parts(steps),
        [VMEM] * 6 + [HBM], slots(2 * steps - early), limit=44)(mine, theirs, index, coupling, *first, inverse)
    home, away = (*first, *rest[:2]), rest[2:]
    term, index, coupling = ordered(term, index, coupling)
    got = swap_core(term)
    high, low = call("spread", spread_kernel, [shape(m, half, dtype=BF16)] * 2, [VMEM, VMEM])(index, coupling)
    term, high, low, got = ordered(term, high, low, got)
    total = term + got

    def back(u, split_inverse):
        out, = call("back", back_kernel, [shape(m + n, half)], [VMEM] * (3 + len(split_inverse)))(
            u, high, low, *split_inverse)
        return out

    total, u = ordered(total, u)
    heard = [swap_leaf(total, *masks) for masks in ((1, 1), (24, 8), (16, 25), (17, 9))]
    sent0 = back(u, away)
    total, sent0, *heard = ordered(total, sent0, *heard)
    total, = call("octet", octet_kernel, [shape(n, m)], [VMEM] * 5)(total, *heard)
    total, sep_inverse, sep_parent, sep_rhs = ordered(total, sep_inverse, sep_parent, sep_rhs)
    got = swap_core(total)
    wayh, wayl, own, chosen = call(
        "tree", tree_kernel, [shape(k, m, dtype=BF16)] * 2 + [shape(5, k, k), shape(n, m + k)],
        [VMEM] * 3)(sep_inverse, sep_parent, sep_rhs)
    total, got, own = ordered(total, got, own)
    total = total + got

    total, u, sent0 = ordered(total, u, sent0)
    received0 = swap_core(sent0)
    heard = [swap_leaf(total, *masks) for masks in ((32, 1), (34, 2), (39, 7), (37, 5))]
    kept0 = back(u, home)
    total, kept0, *heard = ordered(total, kept0, *heard)
    part, = call("pair", pair_kernel, [shape(n, m)], [VMEM] * 5)(total, *heard)
    part, own, sep_inverse, sep_parent = ordered(part, own, sep_inverse, sep_parent)
    got = swap_core(part)
    otherh, otherl, root = call(
        "root", root_kernel, [shape(k, m, dtype=BF16)] * 2 + [shape(k, m)], [VMEM] * 3)(sep_inverse, sep_parent, own)
    part, got, root = ordered(part, got, root)
    source, = call("source", source_kernel, [shape(n, m + k)], [VMEM] * 3)(part, got, chosen)

    source, u, root = ordered(source, u, root)
    other = swap_leaf(source, 96)
    base, lower, qh, ql = call("join", functools.partial(join_kernel, chunk),
                               [shape(n, half), shape(2 * k, half)] + [shape(k, half + m, dtype=BF16)] * 2,
                               [VMEM] * 3)(kept0, received0, root)
    pre, solved, top = call("lower", lower_kernel, [shape(n, half), shape(2, n, k), shape(n, k)], [VMEM] * 7)(
        source, chosen, wayh, wayl, own, base, lower)
    pre, other = ordered(pre, other)
    out, sep = call("last", last_kernel, [shape(n, half), shape(levels, n, k)], [VMEM] * 8)(
        other, otherh, otherl, top, pre, solved, qh, ql)
    return (out[None], sep[None])


def solution(mesh):
    placed = (
        P("leaf", None, "sep"),
        P("leaf", "sep", None),
        P("leaf", None, None),
        P("leaf", None, None, None),
        P(),
        P(),
        P(),
    )
    return jax.shard_map(
        local,
        mesh=mesh,
        in_specs=placed,
        out_specs=(P("leaf", None, "sep"), P("leaf", None, None, None)),
        check_vma=False,
    )
```

```python
import functools

import jax
import jax.numpy as jnp
from jax import lax
from jax.experimental import pallas as pl
from jax.experimental.pallas import tpu as pltpu
from jax.sharding import PartitionSpec as P

F32, BF16 = jnp.float32, jnp.bfloat16
MIB = 1 << 20
VMEM = pl.BlockSpec(memory_space=pltpu.VMEM)
HBM = pl.BlockSpec(memory_space=pltpu.HBM)
NN = (((1,), (0,)), ((), ()))
NT = (((1,), (1,)), ((), ()))
TN = (((0,), (0,)), ((), ()))


def shape(*dims, dtype=F32):
    return jax.ShapeDtypeStruct(dims, dtype)


def dot(a, b, dims=NN):
    return lax.dot_general(a, b, dims, preferred_element_type=F32)


def split(x):
    high = x.astype(BF16)
    return high, (x - high.astype(F32)).astype(BF16)


def product(a, split_b, dims=NN):
    ah, al = split(a)
    bh, bl = split_b
    rows = a.shape[0]
    both = dot(jnp.concatenate([ah, al], axis=0), bh, dims)
    return both[:rows] + both[rows:] + dot(ah, bl, dims)


def call(name, body, outs, ins, scratch=(), limit=24):
    return pl.pallas_call(
        body,
        out_shape=outs,
        in_specs=ins,
        out_specs=[VMEM] * len(outs),
        scratch_shapes=list(scratch),
        compiler_params=pltpu.CompilerParams(vmem_limit_bytes=limit * MIB),
        name=name,
    )


def load_columns(inverse_ref, firsts, chunk, a_ref, sems):
    copies = []
    for s, first in enumerate(firsts):
        start = pl.multiple_of(first, chunk)
        copy = pltpu.make_async_copy(inverse_ref.at[:, pl.ds(start, chunk)], a_ref.at[s], sems.at[s])
        copy.start()
        copies.append(copy)
    return copies


def load_kernel(chunk, inverse_ref, ah_ref, al_ref, a_ref, sems):
    steps, half = ah_ref.shape[:2]
    firsts = [lax.axis_index("sep") * half + s * chunk for s in range(steps)]
    for s, copy in enumerate(load_columns(inverse_ref, firsts, chunk, a_ref, sems)):
        copy.wait()
        ah_ref[s], al_ref[s] = split(a_ref[s])


def paired(x):
    return jnp.concatenate(split(x), axis=0)


def one_hot(index_ref, level, rows, first):
    row = lax.broadcasted_iota(jnp.int32, (rows, index_ref.shape[2]), 0) + first
    return jnp.where(row == index_ref[level], 1.0, 0.0).astype(BF16)


def leaf_kernel(chunk, mine_ref, theirs_ref, index_ref, coupling_ref, eh_ref, el_ref, inverse_ref, term_ref, u_ref, rh_ref, rl_ref, ah_ref, al_ref, a_ref, sems):
    n, half = mine_ref.shape
    levels, _, k = index_ref.shape
    side = lax.axis_index("sep")
    early, rest = eh_ref.shape[0], rh_ref.shape[0]
    firsts = [side * half + (early + s) * chunk for s in range(rest)]
    firsts += [(1 - side) * half + s * chunk for s in range(half // chunk)]
    copies = load_columns(inverse_ref, firsts, chunk, a_ref, sems)
    total = jnp.zeros((2 * n, half), F32)
    for s in range(early):
        x = paired(mine_ref[:, s * chunk:(s + 1) * chunk])
        total = total + (dot(x, eh_ref[s], NT) + dot(x, el_ref[s], NT))
    hot = [one_hot(index_ref, level, half, side * half) for level in range(levels)]
    for s, copy in enumerate(copies):
        mine = s < rest
        x_ref, high_ref, low_ref = (mine_ref, rh_ref, rl_ref) if mine else (theirs_ref, ah_ref, al_ref)
        to = s if mine else s - rest
        at = early + s if mine else to
        x = paired(x_ref[:, at * chunk:(at + 1) * chunk])
        copy.wait()
        ah, al = split(a_ref[s])
        high_ref[to] = ah
        low_ref[to] = al
        total = total + (dot(x, ah, NT) + dot(x, al, NT))
    u = total[:n] + total[n:]
    u_ref[...] = u
    uh, um = split(u)
    ul = (u - uh.astype(F32) - um.astype(F32)).astype(BF16)
    parts = jnp.concatenate([uh, um, ul], axis=0)
    picked = dot(parts, jnp.concatenate(hot, axis=1))
    picked = picked[:n] + picked[n:2 * n] + picked[2 * n:]
    for level in range(levels):
        cols = slice(level * k, (level + 1) * k)
        term_ref[:, cols] = product(picked[:, cols], split(coupling_ref[level]), NT)


def spread_kernel(index_ref, coupling_ref, high_ref, low_ref):
    levels, _, k = index_ref.shape
    half = high_ref.shape[1]
    for level in range(levels):
        hot = one_hot(index_ref, level, half, lax.axis_index("sep") * half)
        ch, cl = split(coupling_ref[level])
        moved = dot(jnp.concatenate([ch, cl], axis=0), hot, NT).astype(BF16)
        high_ref[level * k:(level + 1) * k, :] = moved[:k]
        low_ref[level * k:(level + 1) * k, :] = moved[k:]


def back_kernel(first, last, u_ref, high_ref, low_ref, *refs):
    *refs, out_ref = refs
    n = u_ref.shape[0]
    uh, ul = split(u_ref[...])
    low = low_ref[...]
    left = jnp.concatenate([high_ref[...], uh, ul], axis=0)
    m = low.shape[0]
    chunk = refs[0].shape[2]
    highs, lows = [
        [ref.at[s] for ref in some for s in range(ref.shape[0])] for some in (refs[::2], refs[1::2])
    ]
    for s in range(first, last, 2):
        end = min(s + 2, last)
        cols = slice((s - first) * chunk, (end - first) * chunk)
        ah = jnp.concatenate([ref[...] for ref in highs[s:end]], axis=1)
        al = jnp.concatenate([ref[...] for ref in lows[s:end]], axis=1)
        one = dot(left, ah)
        three = dot(left[:m + n], al)
        out_ref[:m, cols] = one[:m] + dot(low, ah) + three[:m]
        out_ref[m:, cols] = one[m:m + n] + one[m + n:] + three[m:]


def square(x):
    high, low = split(x)
    return dot(high, high, TN) + dot(low, high, TN) + dot(high, low, TN)


def pair_matrices(inverse_ref, parent_ref, near, sibling, middle):
    g0 = product(parent_ref[near], split(inverse_ref[near]))
    gs = product(parent_ref[sibling], split(inverse_ref[sibling]))
    g1 = product(parent_ref[middle], split(inverse_ref[middle]))
    return g0, gs, g1, jnp.concatenate([g1, -product(g1, split(g0)), -product(g1, split(gs))], axis=1)


def tree_kernel(inverse_ref, parent_ref, rhs_ref, wayh_ref, wayl_ref, own_ref, chosen_ref):
    k = inverse_ref.shape[1]
    plane = lax.axis_index("leaf") >> 5
    near, sibling, middle = plane, plane ^ 1, 4 + (plane >> 1)
    g0, gs, g1, way = pair_matrices(inverse_ref, parent_ref, near, sibling, middle)
    wayh_ref[...], wayl_ref[...] = split(way)
    own_ref[0] = g0
    own_ref[1] = gs
    own_ref[2] = square(inverse_ref[near])
    own_ref[3] = square(inverse_ref[middle])
    own_ref[4] = g1
    chosen_ref[:, :k] = rhs_ref[middle]
    chosen_ref[:, k:2 * k] = rhs_ref[near]
    chosen_ref[:, 2 * k:3 * k] = rhs_ref[sibling]
    chosen_ref[:, 3 * k:] = rhs_ref[inverse_ref.shape[0] - 1]


def root_kernel(inverse_ref, parent_ref, own_ref, wayh_ref, wayl_ref, root_ref):
    k = inverse_ref.shape[1]
    plane = 3 - (lax.axis_index("leaf") >> 5)
    way = pair_matrices(inverse_ref, parent_ref, plane, plane ^ 1, 4 + (plane >> 1))[3]
    wayh_ref[...], wayl_ref[...] = split(way)
    h2 = square(inverse_ref[inverse_ref.shape[0] - 1])
    k1 = product(h2, split(own_ref[4]))
    root_ref[:, :k] = product(k1, split(own_ref[0]))
    root_ref[:, k:2 * k] = -k1
    root_ref[:, 2 * k:] = h2


def columns_of(refs, chunk):
    return [ref.at[:, s:s + chunk] for ref in refs for s in range(0, ref.shape[1], chunk)]


def join_kernel(chunk, mine_ref, got0_ref, got1_ref, root_ref, base_ref, low_ref, qh_ref, ql_ref):
    k = root_ref.shape[0]
    root = root_ref[...]
    m = root.shape[1]
    width = base_ref.shape[1]
    pairs = zip(columns_of((mine_ref,), chunk), columns_of((got0_ref, got1_ref), chunk))
    for s, (mine_ref, got_ref) in enumerate(pairs):
        cols = slice(s * chunk, (s + 1) * chunk)
        b = mine_ref[:m, :] + got_ref[:m, :]
        base_ref[:, cols] = mine_ref[m:, :] + got_ref[m:, :]
        low_ref[:, cols] = b[:2 * k]
        qh_ref[:, cols], ql_ref[:, cols] = split(product(root, split(b)))
    qh_ref[:, width:], ql_ref[:, width:] = split(root)


def octet_kernel(total_ref, four_ref, one_ref, two_ref, three_ref, out_ref):
    own = total_ref[...] + four_ref[...]
    first = lax.axis_index("sep") == 0
    out_ref[...] = one_ref[...] + two_ref[...] + three_ref[...] + jnp.where(first, own, 0.0)


def pair_kernel(total_ref, near_ref, two_ref, six_ref, five_ref, out_ref):
    own = jnp.where(lax.axis_index("sep") == 0, total_ref[...], near_ref[...])
    out_ref[...] = own + two_ref[...] + six_ref[...] + five_ref[...]


def source_kernel(part_ref, got_ref, chosen_ref, out_ref):
    k = part_ref.shape[1] // 3
    first = lax.axis_index("sep") == 0
    part, got = part_ref[...], got_ref[...]
    own, other = jnp.where(first, part, got), jnp.where(first, got, part)
    out_ref[:, :k] = chosen_ref[:, :k] - own[:, k:2 * k] - other[:, k:2 * k]
    out_ref[:, k:2 * k] = chosen_ref[:, k:2 * k] - own[:, :k]
    out_ref[:, 2 * k:3 * k] = chosen_ref[:, 2 * k:3 * k] - other[:, :k]
    out_ref[:, 3 * k:] = own[:, 2 * k:] + other[:, 2 * k:]


def lower_kernel(source_ref, chosen_ref, wayh_ref, wayl_ref, own_ref, base_ref, low_ref, pre_ref, solved_ref, top_ref):
    k = own_ref.shape[1]
    t1, s0, sb = source_ref[:, :k], source_ref[:, k:2 * k], source_ref[:, 2 * k:3 * k]
    c0 = product(s0, split(own_ref[2]))
    s1 = t1 - product(s0, split(own_ref[0]), NT) - product(sb, split(own_ref[1]), NT)
    c1 = product(s1, split(own_ref[3]))
    c0 = c0 - product(c1, split(own_ref[0]))
    solved_ref[0] = c0
    solved_ref[1] = c1
    pre_ref[...] = base_ref[...] - product(jnp.concatenate([c0, c1], axis=1), split(low_ref[...]))
    up = product(source_ref[:, :3 * k], (wayh_ref[...], wayl_ref[...]), NT)
    top_ref[...] = chosen_ref[:, 3 * k:] - source_ref[:, 3 * k:] - up


def last_kernel(other_ref, wayh_ref, wayl_ref, top_ref, pre_ref, solved_ref, qh_ref, ql_ref, out_ref, sep_ref):
    k = top_ref.shape[1]
    width = pre_ref.shape[1]
    up = product(other_ref[:, :3 * k], (wayh_ref[...], wayl_ref[...]), NT)
    s2 = top_ref[...] - other_ref[:, 3 * k:] - up
    add = product(s2, (qh_ref[...], ql_ref[...]))
    out_ref[...] = pre_ref[...] - add[:, :width]
    sep_ref[0] = solved_ref[0] + add[:, width:width + k]
    sep_ref[1] = solved_ref[1] + add[:, width + k:width + 2 * k]
    sep_ref[2] = add[:, width + 2 * k:]


def swap_core(x):
    return lax.ppermute(x, "sep", [(0, 1), (1, 0)])


def swap_leaf(x, mask, first_mask=None):
    masks = (mask if first_mask is None else first_mask, mask)
    count = 2 * lax.axis_size("leaf")
    return lax.ppermute(x, ("leaf", "sep"), [(i, i ^ 2 * masks[i % 2]) for i in range(count)])


def ordered(*arrays):
    return lax.optimization_barrier(arrays)


def local(leaf_rhs, leaf_inverse, skeleton_index, leaf_coupling, sep_rhs, sep_inverse, sep_parent):
    mine, coupling = leaf_rhs[0], leaf_coupling[0]
    index = jnp.transpose(skeleton_index, (1, 0, 2))
    inverse = leaf_inverse[0]
    n, half = mine.shape
    levels, _, k = index.shape
    m = levels * k
    chunk = 256
    steps = half // chunk
    early = 1
    slots = lambda count: [pltpu.VMEM((count, half, chunk), F32), pltpu.SemaphoreType.DMA((count,))]
    parts = lambda count: [shape(count, half, chunk, dtype=BF16)] * 2
    theirs = swap_core(mine)
    first = call("load", functools.partial(load_kernel, chunk), parts(early), [HBM], slots(early), limit=51)(inverse)
    term, u, *rest = call(
        "leaf", functools.partial(leaf_kernel, chunk),
        [shape(n, m), shape(n, half)] + parts(steps - early) + parts(steps),
        [VMEM] * 6 + [HBM], slots(2 * steps - early), limit=44)(mine, theirs, index, coupling, *first, inverse)
    home, away = (*first, *rest[:2]), rest[2:]
    term, index, coupling = ordered(term, index, coupling)
    got = swap_core(term)
    high, low = call("spread", spread_kernel, [shape(m, half, dtype=BF16)] * 2, [VMEM, VMEM])(index, coupling)
    term, high, low, got = ordered(term, high, low, got)
    total = term + got

    def back(u, split_inverse, first, last):
        out, = call("back", functools.partial(back_kernel, first, last), [shape(m + n, (last - first) * chunk)],
                    [VMEM] * (3 + len(split_inverse)))(u, high, low, *split_inverse)
        return out

    total, u = ordered(total, u)
    heard = [swap_leaf(total, *masks) for masks in ((1, 1), (24, 8), (16, 25), (17, 9))]
    sent0 = back(u, away, 0, steps - 1)
    total, sent0, *heard = ordered(total, sent0, *heard)
    total, = call("octet", octet_kernel, [shape(n, m)], [VMEM] * 5)(total, *heard)
    total, sep_inverse, sep_parent, sep_rhs = ordered(total, sep_inverse, sep_parent, sep_rhs)
    got = swap_core(total)
    wayh, wayl, own, chosen = call(
        "tree", tree_kernel, [shape(k, m, dtype=BF16)] * 2 + [shape(5, k, k), shape(n, m + k)],
        [VMEM] * 3)(sep_inverse, sep_parent, sep_rhs)
    total, got, own = ordered(total, got, own)
    total = total + got

    total, u, sent0 = ordered(total, u, sent0)
    received0 = swap_core(sent0)
    heard = [swap_leaf(total, *masks) for masks in ((32, 1), (34, 2), (39, 7), (37, 5))]
    sent1 = back(u, away, steps - 1, steps)
    kept0 = back(u, home, 0, steps)
    total, sent1, kept0, *heard = ordered(total, sent1, kept0, *heard)
    part, = call("pair", pair_kernel, [shape(n, m)], [VMEM] * 5)(total, *heard)
    part, own, sep_inverse, sep_parent = ordered(part, own, sep_inverse, sep_parent)
    got = swap_core(part)
    otherh, otherl, root = call(
        "root", root_kernel, [shape(k, m, dtype=BF16)] * 2 + [shape(k, m)], [VMEM] * 3)(sep_inverse, sep_parent, own)
    part, got, root = ordered(part, got, root)
    source, = call("source", source_kernel, [shape(n, m + k)], [VMEM] * 3)(part, got, chosen)

    source, sent1, root = ordered(source, sent1, root)
    other = swap_leaf(source, 96)
    received1 = swap_core(sent1)
    base, lower, qh, ql = call("join", functools.partial(join_kernel, chunk),
                               [shape(n, half), shape(2 * k, half)] + [shape(k, half + m, dtype=BF16)] * 2,
                               [VMEM] * 4)(kept0, received0, received1, root)
    pre, solved, top = call("lower", lower_kernel, [shape(n, half), shape(2, n, k), shape(n, k)], [VMEM] * 7)(
        source, chosen, wayh, wayl, own, base, lower)
    pre, other = ordered(pre, other)
    out, sep = call("last", last_kernel, [shape(n, half), shape(levels, n, k)], [VMEM] * 8)(
        other, otherh, otherl, top, pre, solved, qh, ql)
    return (out[None], sep[None])


def solution(mesh):
    placed = (
        P("leaf", None, "sep"),
        P("leaf", "sep", None),
        P("leaf", None, None),
        P("leaf", None, None, None),
        P(),
        P(),
        P(),
    )
    return jax.shard_map(
        local,
        mesh=mesh,
        in_specs=placed,
        out_specs=(P("leaf", None, "sep"), P("leaf", None, None, None)),
        check_vma=False,
    )
```
